256 devices in a mesh: dp: 16 (over y_lo, z), seq: 16 (over x, y_hi, core).
Axes of the slice: x: 4, y: 4 (y_hi: 2, y_lo: 2; y = y_hi * 2 + y_lo), z: 8, core: 2. Of those that a mesh axis runs over, the one named last changes fastest.
Arguments:
- tokens: bfloat16 [16, 4096, 1536], P('dp', 'seq'), may hold values from -64 to 64
- keep_index: int32 [16, 4096], P('dp', 'seq'), may hold values from 0 to 8191, as said below
- d_out: bfloat16 [16, 4096, 768], P('dp', 'seq'), may hold values from -6 to 6
- w_query: bfloat16 [1536, 768], replicated, may hold values from -0.15625 to 0.15625
- w_kv: bfloat16 [1536, 1536], replicated, may hold values from -0.15625 to 0.15625
- w_merge: float32 [4, 1536], replicated, may hold values from -2.5 to 2.5
Outputs:
- attended: bfloat16 [16, 4096, 768], P('dp', 'seq')
- grad_tokens: bfloat16 [16, 4096, 1536], P('dp', 'seq')
- grad_query_w: float32 [1536, 768], P('seq')
- grad_kv_w: float32 [1536, 1536], P('seq')
- grad_merge: float32 [4, 1536], P(None, 'seq')
The draws below stay inside these ranges and needn't reach their ends.
Inputs may be any that keep to these rules, and one draw needn't show every extreme that they name: `keep_index`: for each image: ascending and distinct; made of whole aligned blocks of 128 positions, 32 of the 64 blocks, the first and the last block always among them.
All inputs are finite; a program needn't handle non-finite values.
Results may differ from the reference program's by a relative error of at most 0.034.
The reference program's roundings to bfloat16 on the way (of `query`, `merged`, `dscore`, `dq` and `dkv`) count: a program that leaves them out, or rounds other values in their place, can miss the bound.
Values may be sent and summed in bfloat16 or wider, within the bound.
No kernel may reach another device: no remote copies, remote signals or barrier semaphores. Data moves between devices by JAX's collectives and lax.ppermute only.
A program may use at most 128 MiB of HBM per device.

```python
import jax
import jax.numpy as jnp
from jax import lax

D = 1536
HEADS = 12
HEAD = 64
TOK_DEV = 256
BLOCK = 128
COARSE_W = 64
HD = 768
TOKENS = 4096
IMAGES = 16
N_SEQ = 16


def draw_tokens(key, part):
    key = jax.random.fold_in(key, 3)
    first = jax.random.fold_in(key, 0)
    shape = (IMAGES, TOKENS, D)
    values = jnp.clip(jax.random.normal(first, shape, jnp.float32), -6.0, 6.0)
    return values.astype(jnp.bfloat16)


def draw_keep_index(key, part):
    key = jax.random.fold_in(key, 7)
    blocks_all = 2 * TOKENS // BLOCK
    blocks_kept = TOKENS // BLOCK

    def one_image(image_key):
        middle = jax.random.permutation(image_key, blocks_all - 2) + 1
        chosen = jnp.concatenate([jnp.zeros((1,), jnp.int32), middle[:blocks_kept - 2].astype(jnp.int32), jnp.full((1,), blocks_all - 1, jnp.int32)])
        chosen = jnp.sort(chosen)
        return (chosen[:, None] * BLOCK + jnp.arange(BLOCK, dtype=jnp.int32)[None, :]).reshape(TOKENS)
    return jax.vmap(one_image)(jax.random.split(key, IMAGES)).astype(jnp.int32)


def level_of(key, dims, pieces, least, top_value):
    gain = 1.0
    for position, shards_of in pieces:
        draws = jax.random.uniform(jax.random.fold_in(jax.random.fold_in(key, 6), position), (shards_of,), jnp.float32, least / len(pieces), top_value / len(pieces))
        gain = gain * jnp.repeat(jnp.exp(draws), dims[position] // shards_of).reshape((-1,) + (1,) * (len(dims) - 1 - position))
    return gain


def noise(key, shape, spread, limit, pieces=(), held_as=jnp.bfloat16):
    level = level_of(key, shape, pieces, -0.22, 0.18) if pieces else 1.0
    drawn = jax.random.normal(key, shape, jnp.float32) * spread * level
    return jnp.minimum(jnp.maximum(drawn, -limit), limit).astype(held_as)


def setup_inputs(seed: int = 0) -> dict:
    seeds = jax.random.split(jax.random.key(seed), 7)
    tokens = draw_tokens(jax.random.fold_in(seeds[6], 71), 0)
    keep_index = draw_keep_index(jax.random.fold_in(seeds[6], 71), 0)
    d_out = noise(seeds[2], (IMAGES, TOKENS, HD), 1.0, 6.0, ((0, 16), (1, 16)))
    w_query = noise(seeds[3], (D, HD), D ** -0.5, 0.15625)
    w_kv = noise(seeds[4], (D, 2 * HD), D ** -0.5, 0.15625)
    w_merge = noise(seeds[5], (4, D), 0.5, 2.5, (), jnp.float32)
    return dict(tokens=tokens, keep_index=keep_index, d_out=d_out, w_query=w_query, w_kv=w_kv, w_merge=w_merge)


def rotate(values, rows, cols, sign):
    count = values.shape[0]
    quarter = HEAD // 4
    parts = values.reshape(count, HEADS, 4, quarter)
    freq = 100.0 ** (-jnp.arange(quarter, dtype=jnp.float32) / quarter)
    row_angle = (rows[:, None] * freq)[:, None, :]
    col_angle = (cols[:, None] * freq)[:, None, :]
    row_cos, row_sin = jnp.cos(row_angle), sign * jnp.sin(row_angle)
    col_cos, col_sin = jnp.cos(col_angle), sign * jnp.sin(col_angle)
    first, second, third, fourth = parts[:, :, 0], parts[:, :, 1], parts[:, :, 2], parts[:, :, 3]
    turned = jnp.stack([first * row_cos - second * row_sin, first * row_sin + second * row_cos,
                        third * col_cos - fourth * col_sin, third * col_sin + fourth * col_cos], axis=2)
    return turned.reshape(count, HEADS * HEAD)


def places(index):
    cell = index // 4
    inner = index % 4
    rows = (2 * (cell // COARSE_W) + inner // 2).astype(jnp.float32)
    cols = (2 * (cell % COARSE_W) + inner % 2).astype(jnp.float32)
    return rows, cols


def key_places(index):
    cell = index[::4] // 4
    rows = (2 * (cell // COARSE_W)).astype(jnp.float32) + 0.5
    cols = (2 * (cell % COARSE_W)).astype(jnp.float32) + 0.5
    return rows, cols


def rounded(values):
    return lax.optimization_barrier(values.astype(jnp.bfloat16)).astype(jnp.float32)


def one_image(inputs, w_query, w_kv, w_merge):
    tokens, index, grad = inputs
    width = HEADS * HEAD
    cells = TOKENS // 4
    scale = HEAD ** -0.5
    query_rows, query_cols = places(index)
    key_rows, key_cols = key_places(index)
    query = rotate(jnp.dot(tokens, w_query, preferred_element_type=jnp.float32), query_rows, query_cols, 1.0).astype(jnp.bfloat16)
    quads = tokens.astype(jnp.float32).reshape(cells, 4, D)
    merged = jnp.sum(quads * w_merge[None], axis=1).astype(jnp.bfloat16)
    keyval = jnp.dot(merged, w_kv, preferred_element_type=jnp.float32)
    key = rotate(keyval[:, :width], key_rows, key_cols, 1.0).astype(jnp.bfloat16)
    value = keyval[:, width:].astype(jnp.bfloat16)
    query_h = query.astype(jnp.float32).reshape(TOKENS, HEADS, HEAD)
    key_h = key.astype(jnp.float32).reshape(cells, HEADS, HEAD)
    value_h = value.astype(jnp.float32).reshape(cells, HEADS, HEAD)
    scores = jnp.einsum('qhd,khd->hqk', query_h, key_h) * scale
    top = jnp.max(scores, axis=-1)
    expo = jnp.exp(scores - top[..., None])
    denom = jnp.sum(expo, axis=-1)
    mixed = jnp.einsum('hqk,khd->hqd', rounded(expo), value_h) / denom[..., None]
    attended = jnp.transpose(mixed, (1, 0, 2)).reshape(TOKENS, width).astype(jnp.bfloat16)
    logsum = top + jnp.log(denom)
    grad_h = grad.astype(jnp.float32).reshape(TOKENS, HEADS, HEAD)
    delta = jnp.sum(attended.astype(jnp.float32).reshape(TOKENS, HEADS, HEAD) * grad_h, axis=-1).T
    prob = jnp.exp(scores - logsum[..., None])
    prob_b = rounded(prob)
    dprob = jnp.einsum('qhd,khd->hqk', grad_h, value_h)
    dscore = rounded(prob * (dprob - delta[..., None]))
    dq_raw = jnp.einsum('hqk,khd->qhd', dscore, key_h).reshape(TOKENS, width) * scale
    dq = rotate(dq_raw, query_rows, query_cols, -1.0).astype(jnp.bfloat16)
    dscore_g = dscore.reshape(HEADS, N_SEQ, TOK_DEV, cells)
    prob_g = prob_b.reshape(HEADS, N_SEQ, TOK_DEV, cells)
    query_g = query_h.reshape(N_SEQ, TOK_DEV, HEADS, HEAD)
    grad_g = grad_h.reshape(N_SEQ, TOK_DEV, HEADS, HEAD)
    dkey_g = jnp.einsum('hgqk,gqhd->gkhd', dscore_g, query_g).reshape(N_SEQ, cells, width) * scale
    dval_g = jnp.einsum('hgqk,gqhd->gkhd', prob_g, grad_g).reshape(N_SEQ, cells, width)
    dkv_sum = jnp.sum(rounded(jnp.concatenate([dkey_g, dval_g], axis=2)), axis=0)
    dkv = jnp.concatenate([rotate(dkv_sum[:, :width], key_rows, key_cols, -1.0), dkv_sum[:, width:]], axis=1).astype(jnp.bfloat16)
    dmerged = jnp.dot(dkv, w_kv.T, preferred_element_type=jnp.float32)
    back = jnp.dot(dq, w_query.T, preferred_element_type=jnp.float32)
    grad_tokens = (back + (w_merge[None] * dmerged[:, None, :]).reshape(TOKENS, D)).astype(jnp.bfloat16)
    tokens_g = tokens.astype(jnp.float32).reshape(N_SEQ, TOK_DEV, D)
    dq_g = dq.astype(jnp.float32).reshape(N_SEQ, TOK_DEV, width)
    merged_g = merged.astype(jnp.float32).reshape(N_SEQ, TOK_DEV // 4, D)
    dkv_g = dkv.astype(jnp.float32).reshape(N_SEQ, TOK_DEV // 4, 2 * width)
    term_q = jnp.sum(rounded(jnp.einsum('gqd,gqe->gde', tokens_g, dq_g)), axis=0)
    term_kv = jnp.sum(rounded(jnp.einsum('gcd,gce->gde', merged_g, dkv_g)), axis=0)
    quads_g = quads.reshape(N_SEQ, TOK_DEV // 4, 4, D)
    dmerged_g = dmerged.reshape(N_SEQ, TOK_DEV // 4, D)
    term_m = jnp.sum(rounded(jnp.einsum('gctd,gcd->gdt', quads_g, dmerged_g)), axis=0)
    return attended, grad_tokens, term_q, term_kv, term_m


def reference(tokens, keep_index, d_out, w_query, w_kv, w_merge):
    results = lax.map(lambda inputs: one_image(inputs, w_query, w_kv, w_merge), (tokens, keep_index, d_out))
    attended, grad_tokens, term_q, term_kv, term_m = results
    return attended, grad_tokens, jnp.sum(term_q, axis=0), jnp.sum(term_kv, axis=0), jnp.sum(term_m, axis=0).T
```

```python
import jax
import jax.numpy as jnp
import numpy as np
from jax import lax
from jax.experimental import pallas as pl
from jax.experimental.pallas import tpu as pltpu
from jax.sharding import PartitionSpec as P

D = 1536
HD = 768
HEADS = 12
HEAD = 64
GROUP = 192
ROWS = 384
TOK = 256
CELLS = 64
MSG = 400
FREQ = (100.0 ** (-np.arange(16, dtype=np.float64) / 16)).astype(np.float32)
F32 = jnp.float32
BF16 = jnp.bfloat16
VMEM_LIMIT = 56 * 1024 * 1024

X_SHIFT = [[(i, (((i >> 2) + k) % 4) * 4 + (i & 3)) for i in range(16)] for k in range(4)]
Y_SWAP = [(i, i ^ 2) for i in range(16)]
CORE_SWAP = [(i, i ^ 1) for i in range(16)]
YLO_SWAP = [(i, i ^ 8) for i in range(16)]
Z_GROUPS = [list(range(8)), list(range(8, 16))]


def params():
    return pltpu.CompilerParams(vmem_limit_bytes=VMEM_LIMIT)


def vmem():
    return pl.BlockSpec(memory_space=pltpu.VMEM)


def smem():
    return pl.BlockSpec(memory_space=pltpu.SMEM)


def mm(a, b, dims=((1,), (0,))):
    return lax.dot_general(a, b, (dims, ((), ())), preferred_element_type=F32)


def lane_tables(row, col, sign):
    lane = lax.broadcasted_iota(jnp.int32, row.shape, 1)
    angle = jnp.where((lane & 63) < 32, row, col)
    even = (lane & 31) < 16
    return jnp.cos(angle), jnp.sin(angle) * jnp.where(even, -sign, sign), even


def turn(u, cos, sin, even):
    swapped = jnp.where(even, pltpu.roll(u, 112, 1), pltpu.roll(u, 16, 1))
    return u * cos + swapped * sin


def merge(tokf, wm_ref, k, cells):
    total = None
    for t in range(4):
        one = tokf[k, pl.ds(t, cells, stride=4), :] * wm_ref[t : t + 1, pl.ds(128 * k, 128)]
        total = one if total is None else total + one
    return total


def keyval_kernel(x_ref, idx_ref, freq_ref, tok_ref, wm_ref, wkv_ref, o0, o1, o2, o3, tokf, merged, part, piece):
    j = pl.program_id(0)

    @pl.when(j == 0)
    def _():
        for k in range(12):
            tokf[k] = tok_ref[:, pl.ds(128 * k, 128)].astype(F32)
            merged[:, pl.ds(128 * k, 128)] = merge(tokf, wm_ref, k, CELLS).astype(BF16)

    part[j] = mm(merged[...], wkv_ref[...])

    @pl.when(j == 5)
    def _():
        i = lax.broadcasted_iota(jnp.int32, (CELLS, 128), 0)
        first = idx_ref[0] // 4
        second = idx_ref[128] // 4
        cell = jnp.where(i < 32, first + i, second + i - 32)
        row = (2 * (cell >> 6)).astype(F32) + 0.5
        col = (2 * (cell & 63)).astype(F32) + 0.5
        cos, sin, even = lane_tables(row * freq_ref[...], col * freq_ref[...], 1.0)
        left = lax.broadcasted_iota(jnp.int32, (CELLS, 128), 1) < 64
        for k in range(6):
            lanes = pl.ds(128 * (k % 2), 128)
            key = turn(part[k // 2, :, lanes], cos, sin, even)
            val = part[3 + k // 2, :, lanes]
            a = jnp.where(left, key, pltpu.roll(val, 64, 1)).astype(BF16)
            b = jnp.where(left, pltpu.roll(key, 64, 1), val).astype(BF16)
            piece[(2 * k) // 3, (2 * k) % 3] = a
            piece[(2 * k + 1) // 3, (2 * k + 1) % 3] = b
        x = x_ref[0]
        for d, out in enumerate((o0, o1, o2, o3)):
            out[...] = piece[(x + d) % 4]


def keyval(xs, index, freq, tokens, w_merge, w_kv):
    out = jax.ShapeDtypeStruct((3, CELLS, 128), BF16)
    whole = lambda shape: pl.BlockSpec(shape, lambda j: (0,) * len(shape))
    return pl.pallas_call(
        keyval_kernel,
        grid=(6,),
        in_specs=[
            smem(),
            smem(),
            whole((1, 128)),
            whole((TOK, D)),
            whole((4, D)),
            pl.BlockSpec((D, 256), lambda j: (0, j)),
        ],
        out_specs=[whole((3, CELLS, 128))] * 4,
        out_shape=[out] * 4,
        scratch_shapes=[
            pltpu.VMEM((12, TOK, 128), F32),
            pltpu.VMEM((CELLS, D), BF16),
            pltpu.VMEM((6, CELLS, 256), F32),
            pltpu.VMEM((4, 3, CELLS, 128), BF16),
        ],
        compiler_params=params(),
        name="keyval",
    )(xs, index, freq, tokens, w_merge, w_kv)


def sub_tables(row, col, freq):
    return (
        jnp.cos(row * freq),
        jnp.sin(row * freq),
        jnp.cos(col * freq),
        jnp.sin(col * freq),
    )


def sub_turn(u, tables, sign):
    rc, rs, cc, cs = tables
    a, b, c, d = u[0:16], u[16:32], u[32:48], u[48:64]
    return jnp.concatenate(
        [
            a * rc - sign * (b * rs),
            sign * (a * rs) + b * rc,
            c * cc - sign * (d * cs),
            sign * (c * cs) + d * cc,
        ],
        axis=0,
    )


def query_kernel(x_ref, idx_ref, freq_ref, tok_ref, wq_ref, do_ref, o0, o1, o2, o3, scr):
    index = idx_ref[...]
    cell = index >> 2
    row = 2 * (cell >> 6) + ((index >> 1) & 1)
    col = 2 * (cell & 63) + (index & 1)
    row = row.astype(F32)
    col = col.astype(F32)
    tables = sub_tables(row, col, freq_ref[...])
    query = mm(tok_ref[...], wq_ref[...]).T
    grad = do_ref[...].astype(F32).T
    line = lax.broadcasted_iota(jnp.int32, (16, TOK), 0)
    place = jnp.where(line == 0, row, jnp.where(line == 1, col, 0.0)).astype(BF16)
    for h in range(HEADS):
        g, k = h // 3, h % 3
        scr[g, pl.ds(64 * k, 64), :] = (sub_turn(query[64 * h : 64 * h + 64], tables, 1.0) * 0.125).astype(BF16)
    for g in range(4):
        scr[g, pl.ds(GROUP, GROUP), :] = grad[GROUP * g : GROUP * g + GROUP].astype(BF16)
        scr[g, pl.ds(2 * GROUP, 16), :] = place
    x = x_ref[0]
    for d, out in enumerate((o0, o1, o2, o3)):
        out[...] = scr[(x + d) % 4]


def queries(xs, index, freq, tokens, w_query, grad):
    out = jax.ShapeDtypeStruct((MSG, TOK), BF16)
    return pl.pallas_call(
        query_kernel,
        in_specs=[smem()] + [vmem()] * 5,
        out_specs=[vmem()] * 4,
        out_shape=[out] * 4,
        scratch_shapes=[pltpu.VMEM((4, MSG, TOK), BF16)],
        compiler_params=params(),
        name="queries",
    )(xs, index, freq, tokens, w_query, grad)


def attention_kernel(
    x_ref, freq_ref, q0, q1, q2, q3, u0, u1, u2, u3, a0, a1, a2, a3, dq_ref, keep_ref, send_ref, kvn, kvt, qd, att, acc
):
    x = x_ref[0]
    for k, u in enumerate((u0, u1, u2, u3)):
        for d in range(4):
            for h in range(3):
                kvn[h, pl.ds(256 * k + 64 * d, 64), :] = u[d, h]
    for h in range(3):
        kvt[h] = kvn[h].astype(F32).T.astype(BF16)
    for d, q in enumerate((q0, q1, q2, q3)):
        qd[d] = q[...]

    def step(i, carry):
        h = i // 4
        p = i % 4
        kv = kvn[h]
        kv_t = kvt[h]
        at = pl.ds(pl.multiple_of(64 * h, 64), 64)
        q = qd[p, at, :]
        do = qd[p, pl.ds(pl.multiple_of(GROUP + 64 * h, 64), 64), :]
        zero = jnp.zeros_like(q)
        q_pad = jnp.concatenate([q, zero], axis=0)
        do_pad = jnp.concatenate([zero, do], axis=0)
        scores = mm(kv, q_pad)
        top = jnp.max(scores, axis=0, keepdims=True)
        expo = jnp.exp(scores - top)
        denom = jnp.sum(expo, axis=0, keepdims=True)
        inv = 1.0 / denom
        mixed = mm(kv_t[64:128], expo.astype(BF16)) * inv
        mixed = mixed.astype(BF16)
        att[p, at, :] = mixed
        delta = jnp.sum(mixed.astype(F32) * do.astype(F32), axis=0, keepdims=True)
        prob = expo * inv
        dprob = mm(kv, do_pad)
        dscore = (prob * (dprob - delta)).astype(BF16)
        dq = mm(kv_t[0:64], dscore) * 0.125
        place = qd[p, pl.ds(2 * GROUP, 16), :].astype(F32)
        tables = sub_tables(place[0:1], place[1:2], freq_ref[...])
        dq_ref[(x + 4 - p) % 4, at, :] = sub_turn(dq, tables, -1.0).astype(BF16)
        part = mm(dscore, q_pad, ((1,), (1,))) + mm(prob.astype(BF16), do_pad, ((1,), (1,)))

        @pl.when(p == 0)
        def _():
            acc[...] = part

        @pl.when(p > 0)
        def _():
            acc[...] += part

        @pl.when(p == 3)
        def _():
            keep_ref[h] = acc[0:512]
            send_ref[h] = acc[512:1024].astype(BF16)

        return carry

    lax.fori_loop(0, 12, step, 0)
    for d, a in enumerate((a0, a1, a2, a3)):
        a[...] = att[d]


def attention(xs, freq, qs, us):
    out = jax.ShapeDtypeStruct((GROUP, TOK), BF16)
    return pl.pallas_call(
        attention_kernel,
        in_specs=[smem()] + [vmem()] * 9,
        out_specs=[vmem()] * 7,
        out_shape=[out] * 4
        + [
            jax.ShapeDtypeStruct((4, GROUP, TOK), BF16),
            jax.ShapeDtypeStruct((3, 512, 128), F32),
            jax.ShapeDtypeStruct((3, 512, 128), BF16),
        ],
        scratch_shapes=[
            pltpu.VMEM((3, 1024, 128), BF16),
            pltpu.VMEM((3, 128, 1024), BF16),
            pltpu.VMEM((4, MSG, TOK), BF16),
            pltpu.VMEM((4, GROUP, TOK), BF16),
            pltpu.VMEM((1024, 128), F32),
        ],
        compiler_params=params(),
        name="attention",
    )(xs, freq, *qs, *us)


def dkv_kernel(x_ref, freq_ref, q0, q1, q2, q3, keep_ref, core_ref, y_ref, out_ref):
    x = x_ref[0]
    i = lax.broadcasted_iota(jnp.int32, (32, 128), 0).astype(F32)
    left = lax.broadcasted_iota(jnp.int32, (32, 128), 1) < 64
    for d, q in enumerate((q0, q1, q2, q3)):
        place = q[pl.ds(2 * GROUP, 16), :].astype(F32)
        for b in range(2):
            row = jnp.broadcast_to(place[0:1, 128 * b : 128 * b + 1], (32, 128)) + 0.5
            col = jnp.broadcast_to(place[1:2, 128 * b : 128 * b + 1], (32, 128)) + 0.5 + 2.0 * i
            cos, sin, even = lane_tables(row * freq_ref[...], col * freq_ref[...], -1.0)
            at = pl.ds(64 * d + 32 * b, 32)
            for h in range(3):
                total = keep_ref[h, at, :] + core_ref[h, at, :].astype(F32) + y_ref[h, at, :].astype(F32)
                total = jnp.where(left, turn(total, cos, sin, even), total)
                out_ref[(x + 4 - d) % 4, h, pl.ds(32 * b, 32), :] = total.astype(BF16)


def finish_dkv(xs, freq, qs, keep, core, y):
    return pl.pallas_call(
        dkv_kernel,
        in_specs=[smem()] + [vmem()] * 8,
        out_specs=vmem(),
        out_shape=jax.ShapeDtypeStruct((4, 3, CELLS, 128), BF16),
        compiler_params=params(),
        name="finish_dkv",
    )(xs, freq, *qs, keep, core, y)


def term_q_kernel(x_ref, t0, t1, t2, t3, d0, d1, d2, d3, out_ref, scr):
    x = x_ref[0]
    toks = (t0, t1, t2, t3)
    for e, dq in enumerate((d0, d1, d2, d3)):
        total = None
        for d in range(4):
            one = mm(dq[(x + 4 - d) % 4], toks[d][...])
            total = one if total is None else total + one
        scr[(x + 4 - e) % 4] = total
    full = jnp.concatenate([scr[0], scr[1], scr[2], scr[3]], axis=0).T
    for r in range(4):
        out_ref[r] = full[96 * r : 96 * r + 96]


def term_q(xs, toks, dqs):
    return pl.pallas_call(
        term_q_kernel,
        in_specs=[smem()] + [vmem()] * 8,
        out_specs=vmem(),
        out_shape=jax.ShapeDtypeStruct((4, 96, HD), F32),
        scratch_shapes=[pltpu.VMEM((4, GROUP, ROWS), F32)],
        compiler_params=params(),
        name="term_q",
    )(xs, *toks, *dqs)


def natural(tiles, rows, put):
    left = lax.broadcasted_iota(jnp.int32, (rows, 128), 1) < 64
    for k in range(6):
        a = tiles(2 * k).astype(F32)
        b = tiles(2 * k + 1).astype(F32)
        put(128 * k, jnp.where(left, a, pltpu.roll(b, 64, 1)).astype(BF16))
        put(HD + 128 * k, jnp.where(left, pltpu.roll(a, 64, 1), b).astype(BF16))


def term_kv_kernel(x_ref, c_ref, t0, t1, t2, t3, k0, k1, k2, k3, tq_ref, wm_ref, wkv_ref, keep_ref, send_ref, m_ref, tokf, tiles, dkv, full):
    x = x_ref[0]
    c = c_ref[0]
    for d, t in enumerate((t0, t1, t2, t3)):
        for k in range(3):
            tokf[k, pl.ds(256 * d, 256), :] = t[:, pl.ds(128 * k, 128)].astype(F32)
    merged = jnp.concatenate([merge(tokf, wm_ref, k, 256) for k in range(3)], axis=1).astype(BF16)
    for e, k in enumerate((k0, k1, k2, k3)):
        group = (x + 4 - e) % 4
        for d in range(4):
            for h in range(3):
                tiles[group * 3 + h, pl.ds(64 * d, 64), :] = k[(x + 4 - d) % 4, h]

    def put(at, value):
        dkv[:, pl.ds(at, 128)] = value

    natural(lambda h: tiles[h], 256, put)
    grad = dkv[...]
    term = mm(merged, grad, ((0,), (0,)))
    for r in range(4):
        full[r, :, pl.ds(0, HD)] = tq_ref[r]
        full[r, :, pl.ds(HD, D)] = term[96 * r : 96 * r + 96]
    for h in range(2):
        keep_ref[h] = full[2 * h + c]
        send_ref[h] = full[2 * h + 1 - c].astype(BF16)
    dmerged = mm(grad, wkv_ref[...], ((1,), (1,)))
    for t in range(4):
        for k in range(3):
            one = dmerged[:, 128 * k : 128 * k + 128] * tokf[k, pl.ds(t, 256, stride=4), :]
            m_ref[t : t + 1, pl.ds(128 * k, 128)] = jnp.sum(one, axis=0, keepdims=True)
    m_ref[4:8, :] = jnp.zeros((4, ROWS), F32)


def term_kv(xs, cs, toks, dkvs, tq, w_merge, w_kv):
    spec = lambda shape: pl.BlockSpec(shape, lambda i, x, c: (0,) * len(shape))
    grid_spec = pltpu.PrefetchScalarGridSpec(
        num_scalar_prefetch=2,
        grid=(1,),
        in_specs=[spec((TOK, ROWS))] * 4
        + [spec((4, 3, CELLS, 128))] * 4
        + [
            spec((4, 96, HD)),
            pl.BlockSpec((4, ROWS), lambda i, x, c: (0, x[0])),
            pl.BlockSpec((ROWS, D), lambda i, x, c: (x[0], 0)),
        ],
        out_specs=[spec((2, 96, HD + D)), spec((2, 96, HD + D)), spec((8, ROWS))],
        scratch_shapes=[
            pltpu.VMEM((3, 1024, 128), F32),
            pltpu.VMEM((12, 256, 128), BF16),
            pltpu.VMEM((256, D), BF16),
            pltpu.VMEM((4, 96, HD + D), F32),
        ],
    )
    return pl.pallas_call(
        term_kv_kernel,
        grid_spec=grid_spec,
        out_shape=[
            jax.ShapeDtypeStruct((2, 96, HD + D), F32),
            jax.ShapeDtypeStruct((2, 96, HD + D), BF16),
            jax.ShapeDtypeStruct((8, ROWS), F32),
        ],
        compiler_params=params(),
        name="term_kv",
    )(xs, cs, *toks, *dkvs, tq, w_merge, w_kv)


def grad_tokens_kernel(x_ref, d0, d1, d2, d3, k0, k1, k2, k3, wq_ref, wkv_ref, wm_ref, out_ref, tiles, dkv, dqs, back):
    x = x_ref[0]
    for e, (q, k) in enumerate(((d0, k0), (d1, k1), (d2, k2), (d3, k3))):
        group = (x + 4 - e) % 4
        dqs[group] = q[0]
        for h in range(3):
            tiles[group * 3 + h] = k[0, h]

    def put(at, value):
        dkv[:, pl.ds(at, 128)] = value

    natural(lambda h: tiles[h], CELLS, put)
    dq = jnp.concatenate([dqs[g].astype(F32).T.astype(BF16) for g in range(4)], axis=1)
    full = mm(dq, wq_ref[...], ((1,), (1,)))
    dmerged = mm(dkv[...], wkv_ref[...], ((1,), (1,)))
    for k in range(12):
        lanes = pl.ds(128 * k, 128)
        back[k] = full[:, 128 * k : 128 * k + 128]
        for t in range(4):
            at = pl.ds(t, CELLS, stride=4)
            back[k, at, :] = back[k, at, :] + wm_ref[t : t + 1, lanes] * dmerged[:, 128 * k : 128 * k + 128]
        out_ref[0, :, lanes] = back[k].astype(BF16)


def grad_of_tokens(xs, dqs, dkvs, w_query, w_kv, w_merge):
    spec = lambda shape: pl.BlockSpec(shape, lambda i, x: (0,) * len(shape))
    grid_spec = pltpu.PrefetchScalarGridSpec(
        num_scalar_prefetch=1,
        grid=(1,),
        in_specs=[pl.BlockSpec((1, GROUP, TOK), lambda i, x: (x[0], 0, 0))] * 4
        + [pl.BlockSpec((1, 3, CELLS, 128), lambda i, x: (x[0], 0, 0, 0))] * 4
        + [spec((D, HD)), spec((D, D)), spec((4, D))],
        out_specs=spec((1, TOK, D)),
        scratch_shapes=[
            pltpu.VMEM((12, CELLS, 128), BF16),
            pltpu.VMEM((CELLS, D), BF16),
            pltpu.VMEM((4, GROUP, TOK), BF16),
            pltpu.VMEM((12, TOK, 128), F32),
        ],
    )
    return pl.pallas_call(
        grad_tokens_kernel,
        grid_spec=grid_spec,
        out_shape=jax.ShapeDtypeStruct((1, TOK, D), BF16),
        compiler_params=params(),
        name="grad_tokens",
    )(xs, *dqs, *dkvs, w_query, w_kv, w_merge)


def spread_x(parts):
    return [parts[0]] + [lax.ppermute(parts[k], "seq", X_SHIFT[k]) for k in range(1, 4)]


def on_device(tokens, keep_index, d_out, w_query, w_kv, w_merge):
    own = tokens[0]
    place = lax.axis_index("seq")
    x = place // 4
    y = (place // 2) % 2
    c = place % 2
    xs = x.reshape(1)
    cs = c.reshape(1)
    lane_freq = jnp.asarray(np.tile(FREQ, 8)[None, :])
    sub_freq = jnp.asarray(np.broadcast_to(FREQ[:, None], (16, TOK)).copy())

    parts = keyval(xs, keep_index[0], lane_freq, own, w_merge, w_kv)
    unit = jnp.stack(spread_x(parts))
    unit_c = lax.ppermute(unit, "seq", CORE_SWAP)
    unit_y = lax.ppermute(unit, "seq", Y_SWAP)
    unit_cy = lax.ppermute(unit_y, "seq", CORE_SWAP)
    qs = spread_x(queries(xs, keep_index, sub_freq, own, w_query, d_out[0]))

    held = lax.optimization_barrier((own, unit_y))[0]
    slices = [lax.dynamic_slice(held, (0, ROWS * ((x + k) % 4)), (TOK, ROWS)) for k in range(4)]
    toks = spread_x(slices)

    a0, a1, a2, a3, dq, keep, send = attention(xs, sub_freq, qs, [unit, unit_y, unit_c, unit_cy])
    core = lax.ppermute(send, "seq", CORE_SWAP)
    other = (keep[:, 256:] + core[:, 256:].astype(F32)).astype(BF16)
    from_y = lax.ppermute(other, "seq", Y_SWAP)
    dqs = [dq] + [lax.ppermute(dq, "seq", X_SHIFT[k]) for k in range(1, 4)]
    dkv = finish_dkv(xs, lane_freq, qs, keep, core, from_y)
    dkvs = [dkv] + [lax.ppermute(dkv, "seq", X_SHIFT[k]) for k in range(1, 4)]

    back = [a0] + [lax.ppermute(a, "seq", X_SHIFT[4 - k]) for k, a in ((1, a1), (2, a2), (3, a3))]
    order = jnp.stack(back)
    att = jnp.concatenate([lax.dynamic_index_in_dim(order, (g + 4 - x) % 4, 0, False) for g in range(4)], axis=0)
    attended = att.T

    tq = term_q(xs, toks, dqs)
    keep, send, m = term_kv(xs, cs, toks, dkvs, tq, w_merge, w_kv)
    got = lax.ppermute(send, "seq", CORE_SWAP)
    m = m + lax.ppermute(m, "seq", CORE_SWAP)
    summed = keep + got.astype(F32)
    mine = lax.dynamic_index_in_dim(summed, y, 0, False)
    theirs = lax.dynamic_index_in_dim(summed, 1 - y, 0, False).astype(BF16)
    got = lax.ppermute(theirs, "seq", Y_SWAP)
    m = m + lax.ppermute(m, "seq", Y_SWAP)
    mine = (mine + got.astype(F32)).astype(BF16)
    chunks = mine.reshape(4, 24, 2, 1152).transpose(0, 2, 1, 3).reshape(8, 24, 1152)
    m = lax.dynamic_slice(m, (0, 96 * (2 * y + c)), (8, 96)).astype(BF16)
    m = jnp.pad(m, ((0, 0), (0, 1152 - 96)))
    chunks = jnp.concatenate([chunks, jnp.broadcast_to(m[None], (8, 8, 1152))], axis=1)
    got = lax.all_to_all(chunks, "dp", 0, 0, axis_index_groups=Z_GROUPS)
    shard = jnp.sum(got.astype(F32), axis=0).astype(BF16)
    pair = lax.ppermute(shard, "dp", YLO_SWAP)
    shard = shard.astype(F32) + pair.astype(F32)
    grad_m = shard[24:28, :96]
    final = shard[:24].astype(BF16)
    final = lax.all_to_all(jnp.broadcast_to(final[None], (8, 24, 1152)), "dp", 0, 0, axis_index_groups=Z_GROUPS)
    final = final.reshape(4, 2, 24, 1152).transpose(0, 2, 1, 3).reshape(96, 2304).astype(F32)

    grads = grad_of_tokens(xs, dqs, dkvs, w_query, w_kv, w_merge)
    return attended[None], grads, final[:, :HD], final[:, HD:], grad_m


def solution(mesh):
    placed = (P("dp", "seq", None), P("dp", "seq"), P("dp", "seq", None), P(), P(), P())
    return jax.shard_map(
        on_device,
        mesh=mesh,
        in_specs=placed,
        out_specs=(
            P("dp", "seq", None),
            P("dp", "seq", None),
            P("seq", None),
            P("seq", None),
            P(None, "seq"),
        ),
        check_vma=False,
    )
```

```python
import jax
import jax.numpy as jnp
import numpy as np
from jax import lax
from jax.experimental import pallas as pl
from jax.experimental.pallas import tpu as pltpu
from jax.sharding import PartitionSpec as P

D = 1536
HD = 768
HEADS = 12
HEAD = 64
GROUP = 192
ROWS = 384
TOK = 256
CELLS = 64
MSG = 400
FREQ = (100.0 ** (-np.arange(16, dtype=np.float64) / 16)).astype(np.float32)
F32 = jnp.float32
BF16 = jnp.bfloat16
VMEM_LIMIT = 56 * 1024 * 1024

X_SHIFT = [[(i, (((i >> 2) + k) % 4) * 4 + (i & 3)) for i in range(16)] for k in range(4)]
Y_SWAP = [(i, i ^ 2) for i in range(16)]
CORE_SWAP = [(i, i ^ 1) for i in range(16)]
YLO_SWAP = [(i, i ^ 8) for i in range(16)]
Z_GROUPS = [list(range(8)), list(range(8, 16))]


def params():
    return pltpu.CompilerParams(vmem_limit_bytes=VMEM_LIMIT)


def cost(us):
    return pl.CostEstimate(flops=int(us * 1.1e9), bytes_accessed=int(us * 1e5), transcendentals=0)


def vmem():
    return pl.BlockSpec(memory_space=pltpu.VMEM)


def smem():
    return pl.BlockSpec(memory_space=pltpu.SMEM)


def mm(a, b, dims=((1,), (0,))):
    return lax.dot_general(a, b, (dims, ((), ())), preferred_element_type=F32)


def lane_tables(row, col, sign):
    lane = lax.broadcasted_iota(jnp.int32, row.shape, 1)
    angle = jnp.where((lane & 63) < 32, row, col)
    even = (lane & 31) < 16
    return jnp.cos(angle), jnp.sin(angle) * jnp.where(even, -sign, sign), even


def turn(u, cos, sin, even):
    swapped = jnp.where(even, pltpu.roll(u, 112, 1), pltpu.roll(u, 16, 1))
    return u * cos + swapped * sin


def merge(tokf, wm_ref, k, cells):
    total = None
    for t in range(4):
        one = tokf[k, pl.ds(t, cells, stride=4), :] * wm_ref[t : t + 1, pl.ds(128 * k, 128)]
        total = one if total is None else total + one
    return total


def keyval_kernel(x_ref, idx_ref, freq_ref, tok_ref, wm_ref, wkv_ref, o0, o1, o2, o3, tokf, merged, weights, piece, sems):
    copies = [pltpu.make_async_copy(wkv_ref.at[:, pl.ds(512 * j, 512)], weights.at[j], sems.at[j]) for j in range(3)]
    for one in copies:
        one.start()
    for k in range(12):
        tokf[k] = tok_ref[:, pl.ds(128 * k, 128)].astype(F32)
        merged[:, pl.ds(128 * k, 128)] = merge(tokf, wm_ref, k, CELLS).astype(BF16)
    i = lax.broadcasted_iota(jnp.int32, (CELLS, 128), 0)
    first = idx_ref[0] // 4
    second = idx_ref[128] // 4
    cell = jnp.where(i < 32, first + i, second + i - 32)
    row = (2 * (cell >> 6)).astype(F32) + 0.5
    col = (2 * (cell & 63)).astype(F32) + 0.5
    cos, sin, even = lane_tables(row * freq_ref[...], col * freq_ref[...], 1.0)
    left = lax.broadcasted_iota(jnp.int32, (CELLS, 128), 1) < 64
    tiles = []
    for j in range(3):
        copies[j].wait()
        part = mm(merged[...], weights[j])
        tiles += [part[:, 128 * k : 128 * k + 128] for k in range(4)]
    for k in range(6):
        key = turn(tiles[k], cos, sin, even)
        val = tiles[6 + k]
        a = jnp.where(left, key, pltpu.roll(val, 64, 1)).astype(BF16)
        b = jnp.where(left, pltpu.roll(key, 64, 1), val).astype(BF16)
        piece[(2 * k) // 3, (2 * k) % 3] = a
        piece[(2 * k + 1) // 3, (2 * k + 1) % 3] = b
    x = x_ref[0]
    for d, out in enumerate((o0, o1, o2, o3)):
        out[...] = piece[(x + d) % 4]


def keyval(xs, index, freq, tokens, w_merge, w_kv):
    out = jax.ShapeDtypeStruct((3, CELLS, 128), BF16)
    return pl.pallas_call(
        keyval_kernel,
        in_specs=[smem(), smem(), vmem(), vmem(), vmem(), pl.BlockSpec(memory_space=pl.ANY)],
        out_specs=[vmem()] * 4,
        out_shape=[out] * 4,
        scratch_shapes=[
            pltpu.VMEM((12, TOK, 128), F32),
            pltpu.VMEM((CELLS, D), BF16),
            pltpu.VMEM((3, D, 512), BF16),
            pltpu.VMEM((4, 3, CELLS, 128), BF16),
            pltpu.SemaphoreType.DMA((3,)),
        ],
        compiler_params=params(),
        cost_estimate=cost(6),
        name="keyval",
    )(xs, index, freq, tokens, w_merge, w_kv)


def sub_tables(row, col, freq):
    return (
        jnp.cos(row * freq),
        jnp.sin(row * freq),
        jnp.cos(col * freq),
        jnp.sin(col * freq),
    )


def sub_turn(u, tables, sign):
    rc, rs, cc, cs = tables
    a, b, c, d = u[0:16], u[16:32], u[32:48], u[48:64]
    return jnp.concatenate(
        [
            a * rc - sign * (b * rs),
            sign * (a * rs) + b * rc,
            c * cc - sign * (d * cs),
            sign * (c * cs) + d * cc,
        ],
        axis=0,
    )


def query_kernel(x_ref, idx_ref, freq_ref, tok_ref, wq_ref, do_ref, o0, o1, o2, o3, scr):
    index = idx_ref[...]
    cell = index >> 2
    row = 2 * (cell >> 6) + ((index >> 1) & 1)
    col = 2 * (cell & 63) + (index & 1)
    row = row.astype(F32)
    col = col.astype(F32)
    tables = sub_tables(row, col, freq_ref[...])
    query = mm(tok_ref[...], wq_ref[...]).T
    same = lax.broadcasted_iota(jnp.int32, (TOK, TOK), 0) == lax.broadcasted_iota(jnp.int32, (TOK, TOK), 1)
    same = jnp.where(same, 1.0, 0.0).astype(BF16)
    grad = [mm(same, do_ref[:, pl.ds(256 * k, 256)], ((1,), (1,))).astype(BF16) for k in range(3)]
    grad = jnp.concatenate(grad, axis=0)
    line = lax.broadcasted_iota(jnp.int32, (16, TOK), 0)
    place = jnp.where(line == 0, row, jnp.where(line == 1, col, 0.0)).astype(BF16)
    for h in range(HEADS):
        g, k = h // 3, h % 3
        scr[g, pl.ds(64 * k, 64), :] = (sub_turn(query[64 * h : 64 * h + 64], tables, 1.0) * 0.125).astype(BF16)
    for g in range(4):
        scr[g, pl.ds(GROUP, GROUP), :] = grad[GROUP * g : GROUP * g + GROUP]
        scr[g, pl.ds(2 * GROUP, 16), :] = place
    x = x_ref[0]
    for d, out in enumerate((o0, o1, o2, o3)):
        out[...] = scr[(x + d) % 4]


def queries(xs, index, freq, tokens, w_query, grad):
    out = jax.ShapeDtypeStruct((MSG, TOK), BF16)
    return pl.pallas_call(
        query_kernel,
        in_specs=[smem()] + [vmem()] * 5,
        out_specs=[vmem()] * 4,
        out_shape=[out] * 4,
        scratch_shapes=[pltpu.VMEM((4, MSG, TOK), BF16)],
        compiler_params=params(),
        cost_estimate=cost(4),
        name="queries",
    )(xs, index, freq, tokens, w_query, grad)


def attention_kernel(
    x_ref, freq_ref, q0, q1, q2, q3, u0, u1, u2, u3, a0, a1, a2, a3, dq_ref, keep_ref, send_ref, kvn, kvt, qd, att, tables
):
    x = x_ref[0]
    for k, u in enumerate((u0, u1, u2, u3)):
        for d in range(4):
            for h in range(3):
                kvn[h, pl.ds(256 * k + 64 * d, 64), :] = u[d, h]
    for h in range(3):
        kvt[h] = kvn[h].astype(F32).T.astype(BF16)
    for d, q in enumerate((q0, q1, q2, q3)):
        qd[d] = q[...]

    for p in range(4):
        place = qd[p, pl.ds(2 * GROUP, 16), :].astype(F32)
        for k, table in enumerate(sub_tables(place[0:1], place[1:2], freq_ref[...])):
            tables[p, pl.ds(16 * k, 16), :] = table

    for h in range(3):
        at = pl.ds(64 * h, 64)
        kv = kvn[h]
        kv_t = kvt[h]
        total = None
        outs = []
        for p in range(4):
            q = qd[p, at, :]
            do = qd[p, pl.ds(GROUP + 64 * h, 64), :]
            zero = jnp.zeros_like(q)
            q_pad = jnp.concatenate([q, zero], axis=0)
            do_pad = jnp.concatenate([zero, do], axis=0)
            scores = mm(kv, q_pad)
            top = jnp.max(scores, axis=0, keepdims=True)
            expo = jnp.exp(scores - top)
            denom = jnp.sum(expo, axis=0, keepdims=True)
            inv = 1.0 / denom
            mixed = mm(kv_t[64:128], expo.astype(BF16)) * inv
            mixed = mixed.astype(BF16)
            delta = jnp.sum(mixed.astype(F32) * do.astype(F32), axis=0, keepdims=True)
            prob = expo * inv
            dprob = mm(kv, do_pad)
            dscore = (prob * (dprob - delta)).astype(BF16)
            dq = mm(kv_t[0:64], dscore) * 0.125
            table = [tables[p, pl.ds(16 * k, 16), :] for k in range(4)]
            outs.append((mixed, sub_turn(dq, table, -1.0).astype(BF16)))
            part = mm(dscore, q_pad, ((1,), (1,))) + mm(prob.astype(BF16), do_pad, ((1,), (1,)))
            total = part if total is None else total + part
        for p, (mixed, dq) in enumerate(outs):
            att[p, at, :] = mixed
            dq_ref[(x + 4 - p) % 4, at, :] = dq
        keep_ref[h] = total[0:512]
        send_ref[h] = total[512:1024].astype(BF16)
    for d, a in enumerate((a0, a1, a2, a3)):
        a[...] = att[d]


def attention(xs, freq, qs, us):
    out = jax.ShapeDtypeStruct((GROUP, TOK), BF16)
    return pl.pallas_call(
        attention_kernel,
        in_specs=[smem()] + [vmem()] * 9,
        out_specs=[vmem()] * 7,
        out_shape=[out] * 4
        + [
            jax.ShapeDtypeStruct((4, GROUP, TOK), BF16),
            jax.ShapeDtypeStruct((3, 512, 128), F32),
            jax.ShapeDtypeStruct((3, 512, 128), BF16),
        ],
        scratch_shapes=[
            pltpu.VMEM((3, 1024, 128), BF16),
            pltpu.VMEM((3, 128, 1024), BF16),
            pltpu.VMEM((4, MSG, TOK), BF16),
            pltpu.VMEM((4, GROUP, TOK), BF16),
            pltpu.VMEM((4, 64, TOK), F32),
        ],
        compiler_params=params(),
        cost_estimate=cost(20),
        name="attention",
    )(xs, freq, *qs, *us)


def table_kernel(freq_ref, q0, q1, q2, q3, cos_ref, sin_ref):
    i = lax.broadcasted_iota(jnp.int32, (32, 128), 0).astype(F32)
    left = lax.broadcasted_iota(jnp.int32, (32, 128), 1) < 64
    for d, q in enumerate((q0, q1, q2, q3)):
        place = q[pl.ds(2 * GROUP, 16), :].astype(F32)
        for b in range(2):
            row = jnp.broadcast_to(place[0:1, 128 * b : 128 * b + 1], (32, 128)) + 0.5
            col = jnp.broadcast_to(place[1:2, 128 * b : 128 * b + 1], (32, 128)) + 0.5 + 2.0 * i
            cos, sin, even = lane_tables(row * freq_ref[...], col * freq_ref[...], -1.0)
            at = pl.ds(64 * d + 32 * b, 32)
            cos_ref[at, :] = jnp.where(left, cos, 1.0)
            sin_ref[at, :] = jnp.where(left, sin, 0.0)


def key_tables(freq, qs):
    out = jax.ShapeDtypeStruct((TOK, 128), F32)
    return pl.pallas_call(
        table_kernel,
        in_specs=[vmem()] * 5,
        out_specs=[vmem()] * 2,
        out_shape=[out] * 2,
        compiler_params=params(),
        cost_estimate=cost(2),
        name="key_tables",
    )(freq, *qs)


def dkv_kernel(x_ref, cos_ref, sin_ref, keep_ref, core_ref, y_ref, out_ref):
    x = x_ref[0]
    even = (lax.broadcasted_iota(jnp.int32, (CELLS, 128), 1) & 31) < 16
    for d in range(4):
        at = pl.ds(64 * d, 64)
        for h in range(3):
            total = keep_ref[h, at, :] + core_ref[h, at, :].astype(F32) + y_ref[h, at, :].astype(F32)
            out_ref[(x + 4 - d) % 4, h] = turn(total, cos_ref[at, :], sin_ref[at, :], even).astype(BF16)


def finish_dkv(xs, tables, keep, core, y):
    half = pl.BlockSpec((3, 256, 128), lambda i: (0, 0, 0))
    return pl.pallas_call(
        dkv_kernel,
        grid=(1,),
        in_specs=[smem(), pl.BlockSpec((TOK, 128), lambda i: (0, 0)), pl.BlockSpec((TOK, 128), lambda i: (0, 0)), half, half, half],
        out_specs=pl.BlockSpec((4, 3, CELLS, 128), lambda i: (0, 0, 0, 0)),
        out_shape=jax.ShapeDtypeStruct((4, 3, CELLS, 128), BF16),
        compiler_params=params(),
        cost_estimate=cost(2),
        name="finish_dkv",
    )(xs, *tables, keep, core, y)


def term_q_kernel(x_ref, c_ref, t0, t1, t2, t3, d0, d1, d2, d3, keep_ref, send_ref, scr, rows):
    x = x_ref[0]
    toks = (t0, t1, t2, t3)
    for e, dq in enumerate((d0, d1, d2, d3)):
        total = None
        for d in range(4):
            one = mm(dq[(x + 4 - d) % 4], toks[d][...])
            total = one if total is None else total + one
        scr[(x + 4 - e) % 4] = total
    full = jnp.concatenate([scr[0], scr[1], scr[2], scr[3]], axis=0).T
    for r in range(4):
        rows[r] = full[96 * r : 96 * r + 96]
    c = c_ref[0]
    for h in range(2):
        keep_ref[h] = rows[2 * h + c]
        send_ref[h] = rows[2 * h + 1 - c].astype(BF16)


def term_q(xs, cs, toks, dqs):
    return pl.pallas_call(
        term_q_kernel,
        in_specs=[smem()] * 2 + [vmem()] * 8,
        out_specs=[vmem()] * 2,
        out_shape=[jax.ShapeDtypeStruct((2, 96, HD), F32), jax.ShapeDtypeStruct((2, 96, HD), BF16)],
        scratch_shapes=[pltpu.VMEM((4, GROUP, ROWS), F32), pltpu.VMEM((4, 96, HD), F32)],
        compiler_params=params(),
        cost_estimate=cost(4),
        name="term_q",
    )(xs, cs, *toks, *dqs)


def natural(tiles, rows, put):
    left = lax.broadcasted_iota(jnp.int32, (rows, 128), 1) < 64
    for k in range(6):
        a = tiles(2 * k).astype(F32)
        b = tiles(2 * k + 1).astype(F32)
        put(128 * k, jnp.where(left, a, pltpu.roll(b, 64, 1)).astype(BF16))
        put(HD + 128 * k, jnp.where(left, pltpu.roll(a, 64, 1), b).astype(BF16))


def term_kv_kernel(x_ref, c_ref, t0, t1, t2, t3, k0, k1, k2, k3, wm_ref, wkv_ref, keep_ref, send_ref, tokf, tiles, dkv, full, m_ref):
    x = x_ref[0]
    c = c_ref[0]
    for d, t in enumerate((t0, t1, t2, t3)):
        for k in range(3):
            tokf[k, pl.ds(256 * d, 256), :] = t[:, pl.ds(128 * k, 128)].astype(F32)
    merged = jnp.concatenate([merge(tokf, wm_ref, k, 256) for k in range(3)], axis=1).astype(BF16)
    for e, k in enumerate((k0, k1, k2, k3)):
        group = (x + 4 - e) % 4
        for d in range(4):
            for h in range(3):
                tiles[group * 3 + h, pl.ds(64 * d, 64), :] = k[(x + 4 - d) % 4, h]

    def put(at, value):
        dkv[:, pl.ds(at, 128)] = value

    natural(lambda h: tiles[h], 256, put)
    grad = dkv[...]
    term = mm(merged, grad, ((0,), (0,)))
    for r in range(4):
        full[r] = term[96 * r : 96 * r + 96]
    for h in range(2):
        keep_ref[h, pl.ds(0, 96), :] = full[2 * h + c]
        send_ref[h, pl.ds(0, 96), :] = full[2 * h + 1 - c].astype(BF16)
    dmerged = mm(grad, wkv_ref[...], ((1,), (1,)))
    for t in range(4):
        for k in range(3):
            one = dmerged[:, 128 * k : 128 * k + 128] * tokf[k, pl.ds(t, 256, stride=4), :]
            m_ref[t : t + 1, pl.ds(128 * k, 128)] = jnp.sum(one, axis=0, keepdims=True)
    m_ref[4:16, :] = jnp.zeros((12, ROWS), F32)
    for h in range(2):
        keep_ref[h, pl.ds(96, 16), :] = jnp.zeros((16, D), F32)
        send_ref[h, pl.ds(96, 16), :] = jnp.zeros((16, D), BF16)
        keep_ref[h, pl.ds(96, 16), pl.ds(0, ROWS)] = m_ref[...]
        send_ref[h, pl.ds(96, 16), pl.ds(0, ROWS)] = m_ref[...].astype(BF16)


def term_kv(xs, cs, toks, dkvs, w_merge, w_kv):
    spec = lambda shape: pl.BlockSpec(shape, lambda i, x, c: (0,) * len(shape))
    grid_spec = pltpu.PrefetchScalarGridSpec(
        num_scalar_prefetch=2,
        grid=(1,),
        in_specs=[spec((TOK, ROWS))] * 4
        + [spec((4, 3, CELLS, 128))] * 4
        + [
            pl.BlockSpec((4, ROWS), lambda i, x, c: (0, x[0])),
            pl.BlockSpec((ROWS, D), lambda i, x, c: (x[0], 0)),
        ],
        out_specs=[spec((2, 112, D)), spec((2, 112, D))],
        scratch_shapes=[
            pltpu.VMEM((3, 1024, 128), F32),
            pltpu.VMEM((12, 256, 128), BF16),
            pltpu.VMEM((256, D), BF16),
            pltpu.VMEM((4, 96, D), F32),
            pltpu.VMEM((16, ROWS), F32),
        ],
    )
    return pl.pallas_call(
        term_kv_kernel,
        grid_spec=grid_spec,
        out_shape=[
            jax.ShapeDtypeStruct((2, 112, D), F32),
            jax.ShapeDtypeStruct((2, 112, D), BF16),
        ],
        compiler_params=params(),
        cost_estimate=cost(5),
        name="term_kv",
    )(xs, cs, *toks, *dkvs, w_merge, w_kv)


def grad_tokens_kernel(x_ref, d0, d1, d2, d3, k0, k1, k2, k3, wq_ref, wkv_ref, wm_ref, out_ref, tiles, dkv, dqs, back):
    x = x_ref[0]
    for e, (q, k) in enumerate(((d0, k0), (d1, k1), (d2, k2), (d3, k3))):
        group = (x + 4 - e) % 4
        dqs[group] = q[0]
        for h in range(3):
            tiles[group * 3 + h] = k[0, h]

    def put(at, value):
        dkv[:, pl.ds(at, 128)] = value

    natural(lambda h: tiles[h], CELLS, put)
    dq = jnp.concatenate([dqs[g].astype(F32).T.astype(BF16) for g in range(4)], axis=1)
    full = mm(dq, wq_ref[...], ((1,), (1,)))
    dmerged = mm(dkv[...], wkv_ref[...], ((1,), (1,)))
    for k in range(12):
        lanes = pl.ds(128 * k, 128)
        back[k] = full[:, 128 * k : 128 * k + 128]
        for t in range(4):
            at = pl.ds(t, CELLS, stride=4)
            back[k, at, :] = back[k, at, :] + wm_ref[t : t + 1, lanes] * dmerged[:, 128 * k : 128 * k + 128]
        out_ref[0, :, lanes] = back[k].astype(BF16)


def grad_of_tokens(xs, dqs, dkvs, w_query, w_kv, w_merge):
    spec = lambda shape: pl.BlockSpec(shape, lambda i, x: (0,) * len(shape))
    grid_spec = pltpu.PrefetchScalarGridSpec(
        num_scalar_prefetch=1,
        grid=(1,),
        in_specs=[pl.BlockSpec((1, GROUP, TOK), lambda i, x: (x[0], 0, 0))] * 4
        + [pl.BlockSpec((1, 3, CELLS, 128), lambda i, x: (x[0], 0, 0, 0))] * 4
        + [spec((D, HD)), spec((D, D)), spec((4, D))],
        out_specs=spec((1, TOK, D)),
        scratch_shapes=[
            pltpu.VMEM((12, CELLS, 128), BF16),
            pltpu.VMEM((CELLS, D), BF16),
            pltpu.VMEM((4, GROUP, TOK), BF16),
            pltpu.VMEM((12, TOK, 128), F32),
        ],
    )
    return pl.pallas_call(
        grad_tokens_kernel,
        grid_spec=grid_spec,
        out_shape=jax.ShapeDtypeStruct((1, TOK, D), BF16),
        compiler_params=params(),
        cost_estimate=cost(6),
        name="grad_tokens",
    )(xs, *dqs, *dkvs, w_query, w_kv, w_merge)


def spread_x(parts):
    return [parts[0]] + [lax.ppermute(parts[k], "seq", X_SHIFT[k]) for k in range(1, 4)]


def after(value, earlier):
    return lax.optimization_barrier((value, earlier))[0]


def core_sum(keep, send, y):
    got = lax.ppermute(send, "seq", CORE_SWAP)
    summed = keep + got.astype(F32)
    mine = lax.dynamic_index_in_dim(summed, y, 0, False)
    theirs = lax.dynamic_index_in_dim(summed, 1 - y, 0, False).astype(BF16)
    return mine, theirs


def on_device(tokens, keep_index, d_out, w_query, w_kv, w_merge):
    own = tokens[0]
    place = lax.axis_index("seq")
    x = place // 4
    y = (place // 2) % 2
    c = place % 2
    xs = x.reshape(1)
    cs = c.reshape(1)
    lane_freq = jnp.asarray(np.tile(FREQ, 8)[None, :])
    sub_freq = jnp.asarray(np.broadcast_to(FREQ[:, None], (16, TOK)).copy())

    parts = keyval(xs, keep_index[0], lane_freq, own, w_merge, w_kv)
    got_kv = spread_x(parts)
    q_parts = queries(xs, keep_index, sub_freq, own, w_query, d_out[0])
    got_kv, q_parts = lax.optimization_barrier((got_kv, q_parts))
    unit = jnp.stack(got_kv)
    qs = spread_x(q_parts)
    unit_c = lax.ppermute(unit, "seq", CORE_SWAP)
    unit_y = lax.ppermute(unit, "seq", Y_SWAP)
    unit_cy = lax.ppermute(unit_y, "seq", CORE_SWAP)

    held = after(own, qs[1])
    slices = [lax.dynamic_slice(held, (0, ROWS * ((x + k) % 4)), (TOK, ROWS)) for k in range(4)]
    toks = spread_x(slices)

    a0, a1, a2, a3, dq, keep, send = attention(xs, sub_freq, qs, [unit, unit_y, unit_c, unit_cy])
    dq, keep, send, toks = lax.optimization_barrier((dq, keep, send, toks))
    dqs = [dq] + [lax.ppermute(dq, "seq", X_SHIFT[k]) for k in range(1, 4)]
    core = lax.ppermute(send, "seq", CORE_SWAP)
    other = (keep[:, 256:] + core[:, 256:].astype(F32)).astype(BF16)
    from_y = lax.ppermute(other, "seq", Y_SWAP)
    tables = key_tables(lane_freq, after(qs, other))
    dkv = finish_dkv(xs, tables, keep, core, from_y)
    dkvs = [dkv] + [lax.ppermute(dkv, "seq", X_SHIFT[k]) for k in range(1, 4)]

    keep_q, send_q = term_q(xs, cs, toks, after(dqs, dkv))
    keep_kv, send_kv = term_kv(xs, cs, toks, after(dkvs, send_q), w_merge, w_kv)

    mine_q, theirs_q = core_sum(keep_q, after(send_q, dkv), y)
    mine, theirs = core_sum(keep_kv, send_kv, y)
    got_q = lax.ppermute(theirs_q, "seq", Y_SWAP)
    got = lax.ppermute(theirs, "seq", Y_SWAP)
    grads = grad_of_tokens(xs, after(dqs, (theirs, theirs_q)), dkvs, w_query, w_kv, w_merge)
    got, got_q = after((got, got_q), grads)
    total = mine + got.astype(F32)
    m = lax.dynamic_slice(total[96:104], (0, 96 * (2 * y + c)), (8, 96)).astype(BF16)
    m = jnp.broadcast_to(jnp.pad(m, ((0, 16), (0, 128 - 96)))[None], (8, 24, 128))
    total = total[:96].astype(BF16).reshape(4, 24, 2, 768).transpose(0, 2, 1, 3).reshape(8, 24, 768)
    total_q = (mine_q + got_q.astype(F32)).astype(BF16)
    total_q = total_q.reshape(4, 24, 2, 384).transpose(0, 2, 1, 3).reshape(8, 24, 384)
    chunks = jnp.concatenate([total_q, total, m], axis=2)
    shards = lax.all_to_all(chunks, "dp", 0, 0, axis_index_groups=Z_GROUPS)
    a1, a2, a3 = after((a1, a2, a3), chunks)
    back = [a0] + [lax.ppermute(a, "seq", X_SHIFT[4 - k]) for k, a in ((1, a1), (2, a2), (3, a3))]
    order = jnp.stack(back)
    att = jnp.concatenate([lax.dynamic_index_in_dim(order, (g + 4 - x) % 4, 0, False) for g in range(4)], axis=0)
    attended = att.T

    shard = jnp.sum(shards.astype(F32), axis=0).astype(BF16)
    pair = lax.ppermute(shard, "dp", YLO_SWAP)
    shard = shard.astype(F32) + pair.astype(F32)
    grad_m = shard[:4, 1152 : 1152 + 96]
    final = shard[:, :1152].astype(BF16)
    final = lax.all_to_all(jnp.broadcast_to(final[None], (8, 24, 1152)), "dp", 0, 0, axis_index_groups=Z_GROUPS)
    final = final.reshape(4, 2, 24, 1152).transpose(0, 2, 1, 3)
    grad_q = final[..., :384].reshape(96, HD).astype(F32)
    grad_kv = final[..., 384:].reshape(96, D).astype(F32)
    return attended[None], grads, grad_q, grad_kv, grad_m


def solution(mesh):
    placed = (P("dp", "seq", None), P("dp", "seq"), P("dp", "seq", None), P(), P(), P())
    return jax.shard_map(
        on_device,
        mesh=mesh,
        in_specs=placed,
        out_specs=(
            P("dp", "seq", None),
            P("dp", "seq", None),
            P("seq", None),
            P("seq", None),
            P(None, "seq"),
        ),
        check_vma=False,
    )
```

```python
import jax
import jax.numpy as jnp
import numpy as np
from jax import lax
from jax.experimental import pallas as pl
from jax.experimental.pallas import tpu as pltpu
from jax.sharding import PartitionSpec as P

D = 1536
HD = 768
HEADS = 12
HEAD = 64
GROUP = 192
ROWS = 384
TOK = 256
CELLS = 64
MSG = 400
FREQ = (100.0 ** (-np.arange(16, dtype=np.float64) / 16)).astype(np.float32)
F32 = jnp.float32
BF16 = jnp.bfloat16

X_SHIFT = [[(i, (((i >> 2) + k) % 4) * 4 + (i & 3)) for i in range(16)] for k in range(4)]
Y_SWAP = [(i, i ^ 2) for i in range(16)]
CORE_SWAP = [(i, i ^ 1) for i in range(16)]
YLO_SWAP = [(i, i ^ 8) for i in range(16)]
Z_GROUPS = [list(range(8)), list(range(8, 16))]


def params(mib):
    return pltpu.CompilerParams(vmem_limit_bytes=mib * 1024 * 1024)


def cost(us):
    return pl.CostEstimate(flops=int(us * 1.1e9), bytes_accessed=int(us * 1e5), transcendentals=0)


def vmem():
    return pl.BlockSpec(memory_space=pltpu.VMEM)


def smem():
    return pl.BlockSpec(memory_space=pltpu.SMEM)


def mm(a, b, dims=((1,), (0,))):
    return lax.dot_general(a, b, (dims, ((), ())), preferred_element_type=F32)


def frequency(shape, axis):
    j = lax.broadcasted_iota(jnp.int32, shape, axis) & 15
    freq = jnp.zeros(shape, F32)
    for k in range(16):
        freq = jnp.where(j == k, float(FREQ[k]), freq)
    return freq


def hbm():
    return pl.BlockSpec(memory_space=pltpu.MemorySpace.HBM)


def lane_tables(row, col, sign):
    lane = lax.broadcasted_iota(jnp.int32, row.shape, 1)
    angle = jnp.where((lane & 63) < 32, row, col)
    even = (lane & 31) < 16
    return jnp.cos(angle), jnp.sin(angle) * jnp.where(even, -sign, sign), even


def turn(u, cos, sin, even):
    swapped = jnp.where(even, pltpu.roll(u, 112, 1), pltpu.roll(u, 16, 1))
    return u * cos + swapped * sin


def merge(tokf, wm_ref, k, cells):
    total = None
    for t in range(4):
        one = tokf[k, pl.ds(t, cells, stride=4), :] * wm_ref[t : t + 1, pl.ds(128 * k, 128)]
        total = one if total is None else total + one
    return total


def keyval_kernel(x_ref, idx_ref, tok_hbm, wm_hbm, wkv_ref, o0, o1, o2, o3, tok_ref, wm_ref, tokf, merged, weights, piece, sems):
    copies = [pltpu.make_async_copy(wkv_ref.at[:, pl.ds(512 * j, 512)], weights.at[j], sems.at[j]) for j in range(3)]
    first = [pltpu.make_async_copy(tok_hbm, tok_ref, sems.at[3]), pltpu.make_async_copy(wm_hbm, wm_ref, sems.at[4])]
    for one in first + copies:
        one.start()
    freq = frequency((1, 128), 1)
    i = lax.broadcasted_iota(jnp.int32, (CELLS, 128), 0)
    start = idx_ref[0] // 4
    second = idx_ref[128] // 4
    cell = jnp.where(i < 32, start + i, second + i - 32)
    row = (2 * (cell >> 6)).astype(F32) + 0.5
    col = (2 * (cell & 63)).astype(F32) + 0.5
    cos, sin, even = lane_tables(row * freq, col * freq, 1.0)
    left = lax.broadcasted_iota(jnp.int32, (CELLS, 128), 1) < 64
    for one in first:
        one.wait()
    for k in range(12):
        tokf[k] = tok_ref[:, pl.ds(128 * k, 128)].astype(F32)
        merged[:, pl.ds(128 * k, 128)] = merge(tokf, wm_ref, k, CELLS).astype(BF16)
    tiles = []
    for j in range(3):
        copies[j].wait()
        part = mm(merged[...], weights[j])
        tiles += [part[:, 128 * k : 128 * k + 128] for k in range(4)]
    for k in range(6):
        key = turn(tiles[k], cos, sin, even)
        val = tiles[6 + k]
        a = jnp.where(left, key, pltpu.roll(val, 64, 1)).astype(BF16)
        b = jnp.where(left, pltpu.roll(key, 64, 1), val).astype(BF16)
        piece[(2 * k) // 3, (2 * k) % 3] = a
        piece[(2 * k + 1) // 3, (2 * k + 1) % 3] = b
    x = x_ref[0]
    for d, out in enumerate((o0, o1, o2, o3)):
        out[...] = piece[(x + d) % 4]


def keyval(xs, index, tokens, w_merge, w_kv):
    out = jax.ShapeDtypeStruct((3, CELLS, 128), BF16)
    return pl.pallas_call(
        keyval_kernel,
        in_specs=[smem(), smem(), hbm(), hbm(), hbm()],
        out_specs=[vmem()] * 4,
        out_shape=[out] * 4,
        scratch_shapes=[
            pltpu.VMEM((TOK, D), BF16),
            pltpu.VMEM((4, D), F32),
            pltpu.VMEM((12, TOK, 128), F32),
            pltpu.VMEM((CELLS, D), BF16),
            pltpu.VMEM((3, D, 512), BF16),
            pltpu.VMEM((4, 3, CELLS, 128), BF16),
            pltpu.SemaphoreType.DMA((5,)),
        ],
        compiler_params=params(56),
        cost_estimate=cost(6),
        name="keyval",
    )(xs, index, tokens, w_merge, w_kv)


def sub_tables(row, col, freq):
    return (
        jnp.cos(row * freq),
        jnp.sin(row * freq),
        jnp.cos(col * freq),
        jnp.sin(col * freq),
    )


def sub_turn(u, tables, sign):
    rc, rs, cc, cs = tables
    a, b, c, d = u[0:16], u[16:32], u[32:48], u[48:64]
    return jnp.concatenate(
        [
            a * rc - sign * (b * rs),
            sign * (a * rs) + b * rc,
            c * cc - sign * (d * cs),
            sign * (c * cs) + d * cc,
        ],
        axis=0,
    )


def query_kernel(x_ref, idx_ref, tok_ref, wq_ref, do_ref, o0, o1, o2, o3, scr):
    index = idx_ref[...]
    cell = index >> 2
    row = 2 * (cell >> 6) + ((index >> 1) & 1)
    col = 2 * (cell & 63) + (index & 1)
    row = row.astype(F32)
    col = col.astype(F32)
    tables = sub_tables(row, col, frequency((16, TOK), 0))
    query = mm(tok_ref[...], wq_ref[...]).T
    same = lax.broadcasted_iota(jnp.int32, (TOK, TOK), 0) == lax.broadcasted_iota(jnp.int32, (TOK, TOK), 1)
    same = jnp.where(same, 1.0, 0.0).astype(BF16)
    grad = [mm(same, do_ref[:, pl.ds(256 * k, 256)], ((1,), (1,))).astype(BF16) for k in range(3)]
    grad = jnp.concatenate(grad, axis=0)
    line = lax.broadcasted_iota(jnp.int32, (16, TOK), 0)
    place = jnp.where(line == 0, row, jnp.where(line == 1, col, 0.0)).astype(BF16)
    for h in range(HEADS):
        g, k = h // 3, h % 3
        scr[g, pl.ds(64 * k, 64), :] = (sub_turn(query[64 * h : 64 * h + 64], tables, 1.0) * 0.125).astype(BF16)
    for g in range(4):
        scr[g, pl.ds(GROUP, GROUP), :] = grad[GROUP * g : GROUP * g + GROUP]
        scr[g, pl.ds(2 * GROUP, 16), :] = place
    x = x_ref[0]
    for d, out in enumerate((o0, o1, o2, o3)):
        out[...] = scr[(x + d) % 4]


def queries(xs, index, tokens, w_query, grad):
    out = jax.ShapeDtypeStruct((MSG, TOK), BF16)
    return pl.pallas_call(
        query_kernel,
        in_specs=[smem()] + [vmem()] * 4,
        out_specs=[vmem()] * 4,
        out_shape=[out] * 4,
        scratch_shapes=[pltpu.VMEM((4, MSG, TOK), BF16)],
        compiler_params=params(8),
        cost_estimate=cost(4),
        name="queries",
    )(xs, index, tokens, w_query, grad)


def attention_kernel(
    x_ref, q0, q1, q2, q3, u0, u1, u2, u3, a0, a1, a2, a3, dq_ref, keep_ref, send_ref, kvn, kvt, qd, att, tables
):
    x = x_ref[0]
    for k, u in enumerate((u0, u1, u2, u3)):
        for d in range(4):
            for h in range(3):
                kvn[h, pl.ds(256 * k + 64 * d, 64), :] = u[d, h]
    for h in range(3):
        kvt[h] = kvn[h].astype(F32).T.astype(BF16)
    for d, q in enumerate((q0, q1, q2, q3)):
        qd[d] = q[...]

    freq = frequency((16, TOK), 0)
    for p in range(4):
        place = qd[p, pl.ds(2 * GROUP, 16), :].astype(F32)
        for k, table in enumerate(sub_tables(place[0:1], place[1:2], freq)):
            tables[p, pl.ds(16 * k, 16), :] = table

    for h in range(3):
        at = pl.ds(64 * h, 64)
        kv = kvn[h]
        kv_t = kvt[h]
        total = None
        outs = []
        for p in range(4):
            q = qd[p, at, :]
            do = qd[p, pl.ds(GROUP + 64 * h, 64), :]
            zero = jnp.zeros_like(q)
            q_pad = jnp.concatenate([q, zero], axis=0)
            do_pad = jnp.concatenate([zero, do], axis=0)
            scores = mm(kv, q_pad)
            top = jnp.max(scores, axis=0, keepdims=True)
            expo = jnp.exp(scores - top)
            denom = jnp.sum(expo, axis=0, keepdims=True)
            inv = 1.0 / denom
            mixed = mm(kv_t[64:128], expo.astype(BF16)) * inv
            mixed = mixed.astype(BF16)
            delta = jnp.sum(mixed.astype(F32) * do.astype(F32), axis=0, keepdims=True)
            prob = expo * inv
            dprob = mm(kv, do_pad)
            dscore = (prob * (dprob - delta)).astype(BF16)
            dq = mm(kv_t[0:64], dscore) * 0.125
            table = [tables[p, pl.ds(16 * k, 16), :] for k in range(4)]
            outs.append((mixed, sub_turn(dq, table, -1.0).astype(BF16)))
            part = mm(dscore, q_pad, ((1,), (1,))) + mm(prob.astype(BF16), do_pad, ((1,), (1,)))
            total = part if total is None else total + part
        for p, (mixed, dq) in enumerate(outs):
            att[p, at, :] = mixed
            dq_ref[(x + 4 - p) % 4, at, :] = dq
        keep_ref[h] = total[0:512]
        send_ref[h] = total[512:1024].astype(BF16)
    for d, a in enumerate((a0, a1, a2, a3)):
        a[...] = att[d]


def attention(xs, qs, us):
    out = jax.ShapeDtypeStruct((GROUP, TOK), BF16)
    return pl.pallas_call(
        attention_kernel,
        in_specs=[smem()] + [vmem()] * 8,
        out_specs=[vmem()] * 7,
        out_shape=[out] * 4
        + [
            jax.ShapeDtypeStruct((4, GROUP, TOK), BF16),
            jax.ShapeDtypeStruct((3, 512, 128), F32),
            jax.ShapeDtypeStruct((3, 512, 128), BF16),
        ],
        scratch_shapes=[
            pltpu.VMEM((3, 1024, 128), BF16),
            pltpu.VMEM((3, 128, 1024), BF16),
            pltpu.VMEM((4, MSG, TOK), BF16),
            pltpu.VMEM((4, GROUP, TOK), BF16),
            pltpu.VMEM((4, 64, TOK), F32),
        ],
        compiler_params=params(56),
        cost_estimate=cost(20),
        name="attention",
    )(xs, *qs, *us)


def table_kernel(q0, q1, q2, q3, cos_ref, sin_ref):
    freq = frequency((1, 128), 1)
    i = lax.broadcasted_iota(jnp.int32, (32, 128), 0).astype(F32)
    left = lax.broadcasted_iota(jnp.int32, (32, 128), 1) < 64
    for d, q in enumerate((q0, q1, q2, q3)):
        place = q[pl.ds(2 * GROUP, 16), :].astype(F32)
        for b in range(2):
            row = jnp.broadcast_to(place[0:1, 128 * b : 128 * b + 1], (32, 128)) + 0.5
            col = jnp.broadcast_to(place[1:2, 128 * b : 128 * b + 1], (32, 128)) + 0.5 + 2.0 * i
            cos, sin, even = lane_tables(row * freq, col * freq, -1.0)
            at = pl.ds(64 * d + 32 * b, 32)
            cos_ref[at, :] = jnp.where(left, cos, 1.0)
            sin_ref[at, :] = jnp.where(left, sin, 0.0)


def key_tables(qs):
    out = jax.ShapeDtypeStruct((TOK, 128), F32)
    return pl.pallas_call(
        table_kernel,
        in_specs=[vmem()] * 4,
        out_specs=[vmem()] * 2,
        out_shape=[out] * 2,
        compiler_params=params(56),
        cost_estimate=cost(2),
        name="key_tables",
    )(*qs)


def dkv_kernel(x_ref, cos_ref, sin_ref, keep_ref, core_ref, y_ref, out_ref):
    x = x_ref[0]
    even = (lax.broadcasted_iota(jnp.int32, (CELLS, 128), 1) & 31) < 16
    for d in range(4):
        at = pl.ds(64 * d, 64)
        for h in range(3):
            total = keep_ref[h, at, :] + core_ref[h, at, :].astype(F32) + y_ref[h, at, :].astype(F32)
            out_ref[(x + 4 - d) % 4, h] = turn(total, cos_ref[at, :], sin_ref[at, :], even).astype(BF16)


def finish_dkv(xs, tables, keep, core, y):
    half = pl.BlockSpec((3, 256, 128), lambda i: (0, 0, 0))
    return pl.pallas_call(
        dkv_kernel,
        grid=(1,),
        in_specs=[smem(), pl.BlockSpec((TOK, 128), lambda i: (0, 0)), pl.BlockSpec((TOK, 128), lambda i: (0, 0)), half, half, half],
        out_specs=pl.BlockSpec((4, 3, CELLS, 128), lambda i: (0, 0, 0, 0)),
        out_shape=jax.ShapeDtypeStruct((4, 3, CELLS, 128), BF16),
        compiler_params=params(56),
        cost_estimate=cost(2),
        name="finish_dkv",
    )(xs, *tables, keep, core, y)


def term_q_kernel(x_ref, c_ref, t0, t1, t2, t3, d0, d1, d2, d3, wm_ref, keep_ref, send_ref, tokf, merged_ref, scr, rows):
    x = x_ref[0]
    toks = (t0, t1, t2, t3)
    for d, t in enumerate(toks):
        for k in range(3):
            tokf[k, pl.ds(256 * d, 256), :] = t[:, pl.ds(128 * k, 128)].astype(F32)
    merged_ref[...] = jnp.concatenate([merge(tokf, wm_ref, k, 256) for k in range(3)], axis=1).astype(BF16)
    for e, dq in enumerate((d0, d1, d2, d3)):
        total = None
        for d in range(4):
            one = mm(dq[(x + 4 - d) % 4], toks[d][...])
            total = one if total is None else total + one
        scr[(x + 4 - e) % 4] = total
    full = jnp.concatenate([scr[0], scr[1], scr[2], scr[3]], axis=0).T
    for r in range(4):
        rows[r] = full[96 * r : 96 * r + 96]
    c = c_ref[0]
    for h in range(2):
        keep_ref[h] = rows[2 * h + c]
        send_ref[h] = rows[2 * h + 1 - c].astype(BF16)


def term_q(xs, cs, toks, dqs, w_merge):
    return pl.pallas_call(
        term_q_kernel,
        in_specs=[smem()] * 2 + [vmem()] * 9,
        out_specs=[vmem()] * 4,
        out_shape=[
            jax.ShapeDtypeStruct((2, 96, HD), F32),
            jax.ShapeDtypeStruct((2, 96, HD), BF16),
            jax.ShapeDtypeStruct((3, 1024, 128), F32),
            jax.ShapeDtypeStruct((TOK, ROWS), BF16),
        ],
        scratch_shapes=[pltpu.VMEM((4, GROUP, ROWS), F32), pltpu.VMEM((4, 96, HD), F32)],
        compiler_params=params(12),
        cost_estimate=cost(4),
        name="term_q",
    )(xs, cs, *toks, *dqs, w_merge)


def natural(tiles, rows, put):
    left = lax.broadcasted_iota(jnp.int32, (rows, 128), 1) < 64
    for k in range(6):
        a = tiles(2 * k).astype(F32)
        b = tiles(2 * k + 1).astype(F32)
        put(128 * k, jnp.where(left, a, pltpu.roll(b, 64, 1)).astype(BF16))
        put(HD + 128 * k, jnp.where(left, pltpu.roll(a, 64, 1), b).astype(BF16))


def term_kv_kernel(x_ref, c_ref, tokf, merged_ref, k0, k1, k2, k3, wkv_ref, keep_ref, send_ref, tiles, dkv, full, m_ref):
    x = x_ref[0]
    c = c_ref[0]
    for e, k in enumerate((k0, k1, k2, k3)):
        group = (x + 4 - e) % 4
        for d in range(4):
            for h in range(3):
                tiles[group * 3 + h, pl.ds(64 * d, 64), :] = k[(x + 4 - d) % 4, h]

    def put(at, value):
        dkv[:, pl.ds(at, 128)] = value

    natural(lambda h: tiles[h], 256, put)
    grad = dkv[...]
    term = mm(merged_ref[...], grad, ((0,), (0,)))
    for r in range(4):
        full[r, :, pl.ds(0, D)] = term[96 * r : 96 * r + 96]
    dmerged = mm(grad, wkv_ref[...], ((1,), (1,)))
    for t in range(4):
        for k in range(3):
            one = dmerged[:, 128 * k : 128 * k + 128] * tokf[k, pl.ds(t, 256, stride=4), :]
            m_ref[t : t + 1, pl.ds(128 * k, 128)] = jnp.sum(one, axis=0, keepdims=True)
    m_ref[4:8, :] = jnp.zeros((4, ROWS), F32)
    m = m_ref[...]
    for r in range(4):
        full[r, :, pl.ds(D, 128)] = jnp.zeros((96, 128), F32)
        full[r, pl.ds(0, 8), pl.ds(D, 128)] = jnp.concatenate([m[:, 96 * r : 96 * r + 96], jnp.zeros((8, 32), F32)], axis=1)
    for h in range(2):
        keep_ref[h] = full[2 * h + c]
        send_ref[h] = full[2 * h + 1 - c].astype(BF16)


def term_kv(xs, cs, tokf, merged, dkvs, w_kv):
    spec = lambda shape: pl.BlockSpec(shape, lambda i, x, c: (0,) * len(shape))
    grid_spec = pltpu.PrefetchScalarGridSpec(
        num_scalar_prefetch=2,
        grid=(1,),
        in_specs=[spec((3, 1024, 128)), spec((TOK, ROWS))]
        + [spec((4, 3, CELLS, 128))] * 4
        + [spec((ROWS, D))],
        out_specs=[spec((2, 96, D + 128)), spec((2, 96, D + 128))],
        scratch_shapes=[
            pltpu.VMEM((12, 256, 128), BF16),
            pltpu.VMEM((256, D), BF16),
            pltpu.VMEM((4, 96, D + 128), F32),
            pltpu.VMEM((8, ROWS), F32),
        ],
    )
    return pl.pallas_call(
        term_kv_kernel,
        grid_spec=grid_spec,
        out_shape=[
            jax.ShapeDtypeStruct((2, 96, D + 128), F32),
            jax.ShapeDtypeStruct((2, 96, D + 128), BF16),
        ],
        compiler_params=params(11),
        cost_estimate=cost(5),
        name="term_kv",
    )(xs, cs, tokf, merged, *dkvs, w_kv)


def grad_tokens_kernel(x_ref, d0, d1, d2, d3, k0, k1, k2, k3, wq_ref, wkv_ref, wm_ref, out_ref, tiles, dkv, dqs, back):
    x = x_ref[0]
    for e, (q, k) in enumerate(((d0, k0), (d1, k1), (d2, k2), (d3, k3))):
        group = (x + 4 - e) % 4
        dqs[group] = q[0]
        for h in range(3):
            tiles[group * 3 + h] = k[0, h]

    def put(at, value):
        dkv[:, pl.ds(at, 128)] = value

    natural(lambda h: tiles[h], CELLS, put)
    dq = jnp.concatenate([dqs[g].astype(F32).T.astype(BF16) for g in range(4)], axis=1)
    full = mm(dq, wq_ref[...], ((1,), (1,)))
    dmerged = mm(dkv[...], wkv_ref[...], ((1,), (1,)))
    for k in range(12):
        lanes = pl.ds(128 * k, 128)
        back[k] = full[:, 128 * k : 128 * k + 128]
        for t in range(4):
            at = pl.ds(t, CELLS, stride=4)
            back[k, at, :] = back[k, at, :] + wm_ref[t : t + 1, lanes] * dmerged[:, 128 * k : 128 * k + 128]
        out_ref[0, :, lanes] = back[k].astype(BF16)


def grad_of_tokens(xs, dqs, dkvs, w_query, w_kv, w_merge):
    spec = lambda shape: pl.BlockSpec(shape, lambda i, x: (0,) * len(shape))
    grid_spec = pltpu.PrefetchScalarGridSpec(
        num_scalar_prefetch=1,
        grid=(1,),
        in_specs=[pl.BlockSpec((1, GROUP, TOK), lambda i, x: (x[0], 0, 0))] * 4
        + [pl.BlockSpec((1, 3, CELLS, 128), lambda i, x: (x[0], 0, 0, 0))] * 4
        + [spec((D, HD)), spec((D, D)), spec((4, D))],
        out_specs=spec((1, TOK, D)),
        scratch_shapes=[
            pltpu.VMEM((12, CELLS, 128), BF16),
            pltpu.VMEM((CELLS, D), BF16),
            pltpu.VMEM((4, GROUP, TOK), BF16),
            pltpu.VMEM((12, TOK, 128), F32),
        ],
    )
    return pl.pallas_call(
        grad_tokens_kernel,
        grid_spec=grid_spec,
        out_shape=jax.ShapeDtypeStruct((1, TOK, D), BF16),
        compiler_params=params(56),
        cost_estimate=cost(6),
        name="grad_tokens",
    )(xs, *dqs, *dkvs, w_query, w_kv, w_merge)


def spread_x(parts):
    return [parts[0]] + [lax.ppermute(parts[k], "seq", X_SHIFT[k]) for k in range(1, 4)]


def after(value, earlier):
    return lax.optimization_barrier((value, earlier))[0]


def core_sum(keep, send, y):
    got = lax.ppermute(send, "seq", CORE_SWAP)
    summed = keep + got.astype(F32)
    mine = lax.dynamic_index_in_dim(summed, y, 0, False)
    theirs = lax.dynamic_index_in_dim(summed, 1 - y, 0, False).astype(BF16)
    return mine, theirs


def on_device(tokens, keep_index, d_out, w_query, w_kv, w_merge):
    own = tokens[0]
    place = lax.axis_index("seq")
    x = place // 4
    y = (place // 2) % 2
    c = place % 2
    xs = x.reshape(1)
    cs = c.reshape(1)
    parts = keyval(xs, keep_index[0], own, w_merge, w_kv)
    got_kv = spread_x(parts)
    q_parts = queries(xs, keep_index, own, w_query, d_out[0])
    got_kv, q_parts = lax.optimization_barrier((got_kv, q_parts))
    unit = jnp.stack(got_kv)
    qs = spread_x(q_parts)
    unit_c = lax.ppermute(unit, "seq", CORE_SWAP)
    unit_y = lax.ppermute(unit, "seq", Y_SWAP)
    unit_cy = lax.ppermute(unit_y, "seq", CORE_SWAP)

    held = after(own, qs[1])
    slices = [lax.dynamic_slice(held, (0, ROWS * ((x + k) % 4)), (TOK, ROWS)) for k in range(4)]
    toks = spread_x(slices)

    a0, a1, a2, a3, dq, keep, send = attention(xs, qs, [unit, unit_y, unit_c, unit_cy])
    dq, keep, send, toks = lax.optimization_barrier((dq, keep, send, toks))
    dqs = [dq] + [lax.ppermute(dq, "seq", X_SHIFT[k]) for k in range(1, 4)]
    core = lax.ppermute(send, "seq", CORE_SWAP)
    other = (keep[:, 256:] + core[:, 256:].astype(F32)).astype(BF16)
    from_y = lax.ppermute(other, "seq", Y_SWAP)
    taps, weights = after((w_merge, w_kv), other)
    taps = lax.dynamic_slice(taps, (0, ROWS * x), (4, ROWS))
    weights = lax.dynamic_slice(weights, (ROWS * x, 0), (ROWS, D))
    tables = key_tables(after(qs, other))
    dkv = finish_dkv(xs, tables, keep, core, from_y)
    dkvs = [dkv] + [lax.ppermute(dkv, "seq", X_SHIFT[k]) for k in range(1, 4)]

    keep_q, send_q, tokf, unit_merged = term_q(xs, cs, toks, after(dqs, dkv), taps)
    keep_kv, send_kv = term_kv(xs, cs, tokf, unit_merged, dkvs, weights)
    mine_q, theirs_q = core_sum(keep_q, after(send_q, dkv), y)

    mine, theirs = core_sum(keep_kv, send_kv, y)
    theirs_q = after(theirs_q, theirs)
    got_q = lax.ppermute(theirs_q, "seq", Y_SWAP)
    got = lax.ppermute(theirs, "seq", Y_SWAP)
    grads = grad_of_tokens(xs, after(dqs, (theirs, theirs_q)), dkvs, w_query, w_kv, w_merge)
    got, got_q = after((got, got_q), grads)
    total = mine + got.astype(F32)
    total = total.astype(BF16)
    m = jnp.broadcast_to(total[None, :24, D:], (8, 24, 128))
    total = total[:, :D].reshape(4, 24, 2, 768).transpose(0, 2, 1, 3).reshape(8, 24, 768)
    total_q = (mine_q + got_q.astype(F32)).astype(BF16)
    total_q = total_q.reshape(4, 24, 2, 384).transpose(0, 2, 1, 3).reshape(8, 24, 384)
    chunks = jnp.concatenate([total_q, total, m], axis=2)
    shards = lax.all_to_all(chunks, "dp", 0, 0, axis_index_groups=Z_GROUPS)
    a1, a2, a3 = after((a1, a2, a3), chunks)
    back = [a0] + [lax.ppermute(a, "seq", X_SHIFT[4 - k]) for k, a in ((1, a1), (2, a2), (3, a3))]
    order = jnp.stack(back)
    att = jnp.concatenate([lax.dynamic_index_in_dim(order, (g + 4 - x) % 4, 0, False) for g in range(4)], axis=0)
    attended = att.T

    shard = jnp.sum(shards.astype(F32), axis=0).astype(BF16)
    pair = lax.ppermute(shard, "dp", YLO_SWAP)
    shard = shard.astype(F32) + pair.astype(F32)
    grad_m = shard[:4, 1152 : 1152 + 96]
    final = shard[:, :1152].astype(BF16)
    final = lax.all_to_all(jnp.broadcast_to(final[None], (8, 24, 1152)), "dp", 0, 0, axis_index_groups=Z_GROUPS)
    final = final.reshape(4, 2, 24, 1152).transpose(0, 2, 1, 3)
    grad_q = final[..., :384].reshape(96, HD).astype(F32)
    grad_kv = final[..., 384:].reshape(96, D).astype(F32)
    return attended[None], grads, grad_q, grad_kv, grad_m


def solution(mesh):
    placed = (P("dp", "seq", None), P("dp", "seq"), P("dp", "seq", None), P(), P(), P())
    return jax.shard_map(
        on_device,
        mesh=mesh,
        in_specs=placed,
        out_specs=(
            P("dp", "seq", None),
            P("dp", "seq", None),
            P("seq", None),
            P("seq", None),
            P(None, "seq"),
        ),
        check_vma=False,
    )
```

```python
import jax
import jax.numpy as jnp
import numpy as np
from jax import lax
from jax.experimental import pallas as pl
from jax.experimental.pallas import tpu as pltpu
from jax.sharding import PartitionSpec as P

D = 1536
HD = 768
HEADS = 12
HEAD = 64
GROUP = 192
ROWS = 384
TOK = 256
CELLS = 64
MSG = 400
FREQ = (100.0 ** (-np.arange(16, dtype=np.float64) / 16)).astype(np.float32)
F32 = jnp.float32
BF16 = jnp.bfloat16

X_SHIFT = [[(i, (((i >> 2) + k) % 4) * 4 + (i & 3)) for i in range(16)] for k in range(4)]
Y_SWAP = [(i, i ^ 2) for i in range(16)]
CORE_SWAP = [(i, i ^ 1) for i in range(16)]
YLO_SWAP = [(i, i ^ 8) for i in range(16)]
Z_GROUPS = [list(range(8)), list(range(8, 16))]


def params(mib):
    return pltpu.CompilerParams(vmem_limit_bytes=mib * 1024 * 1024)


def cost(us):
    return pl.CostEstimate(flops=int(us * 1.1e9), bytes_accessed=int(us * 1e5), transcendentals=0)


def vmem():
    return pl.BlockSpec(memory_space=pltpu.VMEM)


def smem():
    return pl.BlockSpec(memory_space=pltpu.SMEM)


def mm(a, b, dims=((1,), (0,))):
    return lax.dot_general(a, b, (dims, ((), ())), preferred_element_type=F32)


def frequency(shape, axis):
    j = lax.broadcasted_iota(jnp.int32, shape, axis) & 15
    freq = jnp.zeros(shape, F32)
    for k in range(16):
        freq = jnp.where(j == k, float(FREQ[k]), freq)
    return freq


def hbm():
    return pl.BlockSpec(memory_space=pltpu.MemorySpace.HBM)


def lane_tables(row, col, sign):
    lane = lax.broadcasted_iota(jnp.int32, row.shape, 1)
    angle = jnp.where((lane & 63) < 32, row, col)
    even = (lane & 31) < 16
    return jnp.cos(angle), jnp.sin(angle) * jnp.where(even, -sign, sign), even


def turn(u, cos, sin, even):
    swapped = jnp.where(even, pltpu.roll(u, 112, 1), pltpu.roll(u, 16, 1))
    return u * cos + swapped * sin


def merge(tokf, wm_ref, k, cells):
    total = None
    for t in range(4):
        one = tokf[k, pl.ds(t, cells, stride=4), :] * wm_ref[t : t + 1, pl.ds(128 * k, 128)]
        total = one if total is None else total + one
    return total


def keyval_kernel(x_ref, idx_ref, tok_hbm, wm_hbm, wkv_ref, o0, o1, o2, o3, tok_ref, wm_ref, tokf, merged, weights, piece, sems):
    copies = [pltpu.make_async_copy(wkv_ref.at[:, pl.ds(512 * j, 512)], weights.at[j], sems.at[j]) for j in range(3)]
    first = [pltpu.make_async_copy(tok_hbm, tok_ref, sems.at[3]), pltpu.make_async_copy(wm_hbm, wm_ref, sems.at[4])]
    for one in first + copies:
        one.start()
    freq = frequency((1, 128), 1)
    i = lax.broadcasted_iota(jnp.int32, (CELLS, 128), 0)
    start = idx_ref[0] // 4
    second = idx_ref[128] // 4
    cell = jnp.where(i < 32, start + i, second + i - 32)
    row = (2 * (cell >> 6)).astype(F32) + 0.5
    col = (2 * (cell & 63)).astype(F32) + 0.5
    cos, sin, even = lane_tables(row * freq, col * freq, 1.0)
    left = lax.broadcasted_iota(jnp.int32, (CELLS, 128), 1) < 64
    for one in first:
        one.wait()
    for k in range(12):
        tokf[k] = tok_ref[:, pl.ds(128 * k, 128)].astype(F32)
        merged[:, pl.ds(128 * k, 128)] = merge(tokf, wm_ref, k, CELLS).astype(BF16)
    tiles = []
    for j in range(3):
        copies[j].wait()
        part = mm(merged[...], weights[j])
        tiles += [part[:, 128 * k : 128 * k + 128] for k in range(4)]
    for k in range(6):
        key = turn(tiles[k], cos, sin, even)
        val = tiles[6 + k]
        a = jnp.where(left, key, pltpu.roll(val, 64, 1)).astype(BF16)
        b = jnp.where(left, pltpu.roll(key, 64, 1), val).astype(BF16)
        piece[(2 * k) // 3, (2 * k) % 3] = a
        piece[(2 * k + 1) // 3, (2 * k + 1) % 3] = b
    x = x_ref[0]
    for d, out in enumerate((o0, o1, o2, o3)):
        out[...] = piece[(x + d) % 4]


def keyval(xs, index, tokens, w_merge, w_kv):
    out = jax.ShapeDtypeStruct((3, CELLS, 128), BF16)
    return pl.pallas_call(
        keyval_kernel,
        in_specs=[smem(), smem(), hbm(), hbm(), hbm()],
        out_specs=[vmem()] * 4,
        out_shape=[out] * 4,
        scratch_shapes=[
            pltpu.VMEM((TOK, D), BF16),
            pltpu.VMEM((4, D), F32),
            pltpu.VMEM((12, TOK, 128), F32),
            pltpu.VMEM((CELLS, D), BF16),
            pltpu.VMEM((3, D, 512), BF16),
            pltpu.VMEM((4, 3, CELLS, 128), BF16),
            pltpu.SemaphoreType.DMA((5,)),
        ],
        compiler_params=params(56),
        cost_estimate=cost(6),
        name="keyval",
    )(xs, index, tokens, w_merge, w_kv)


def sub_tables(row, col, freq):
    return (
        jnp.cos(row * freq),
        jnp.sin(row * freq),
        jnp.cos(col * freq),
        jnp.sin(col * freq),
    )


def sub_turn(u, tables, sign):
    rc, rs, cc, cs = tables
    a, b, c, d = u[0:16], u[16:32], u[32:48], u[48:64]
    return jnp.concatenate(
        [
            a * rc - sign * (b * rs),
            sign * (a * rs) + b * rc,
            c * cc - sign * (d * cs),
            sign * (c * cs) + d * cc,
        ],
        axis=0,
    )


def query_kernel(x_ref, idx_ref, tok_ref, wq_ref, do_ref, o0, o1, o2, o3, scr):
    index = idx_ref[...]
    cell = index >> 2
    row = 2 * (cell >> 6) + ((index >> 1) & 1)
    col = 2 * (cell & 63) + (index & 1)
    row = row.astype(F32)
    col = col.astype(F32)
    tables = sub_tables(row, col, frequency((16, TOK), 0))
    query = mm(tok_ref[...], wq_ref[...]).T
    same = lax.broadcasted_iota(jnp.int32, (TOK, TOK), 0) == lax.broadcasted_iota(jnp.int32, (TOK, TOK), 1)
    same = jnp.where(same, 1.0, 0.0).astype(BF16)
    grad = [mm(same, do_ref[:, pl.ds(256 * k, 256)], ((1,), (1,))).astype(BF16) for k in range(3)]
    grad = jnp.concatenate(grad, axis=0)
    line = lax.broadcasted_iota(jnp.int32, (16, TOK), 0)
    place = jnp.where(line == 0, row, jnp.where(line == 1, col, 0.0)).astype(BF16)
    for h in range(HEADS):
        g, k = h // 3, h % 3
        scr[g, pl.ds(64 * k, 64), :] = (sub_turn(query[64 * h : 64 * h + 64], tables, 1.0) * 0.125).astype(BF16)
    for g in range(4):
        scr[g, pl.ds(GROUP, GROUP), :] = grad[GROUP * g : GROUP * g + GROUP]
        scr[g, pl.ds(2 * GROUP, 16), :] = place
    x = x_ref[0]
    for d, out in enumerate((o0, o1, o2, o3)):
        out[...] = scr[(x + d) % 4]


def queries(xs, index, tokens, w_query, grad):
    out = jax.ShapeDtypeStruct((MSG, TOK), BF16)
    return pl.pallas_call(
        query_kernel,
        in_specs=[smem()] + [vmem()] * 4,
        out_specs=[vmem()] * 4,
        out_shape=[out] * 4,
        scratch_shapes=[pltpu.VMEM((4, MSG, TOK), BF16)],
        compiler_params=params(8),
        cost_estimate=cost(4),
        name="queries",
    )(xs, index, tokens, w_query, grad)


def attention_kernel(
    x_ref, q0, q1, q2, q3, u0, u1, u2, u3, a0, a1, a2, a3, dq_ref, keep_ref, send_ref, kvn, kvt, qd, att, tables
):
    x = x_ref[0]
    for k, u in enumerate((u0, u1, u2, u3)):
        for d in range(4):
            for h in range(3):
                kvn[h, pl.ds(256 * k + 64 * d, 64), :] = u[d, h]
    for h in range(3):
        kvt[h] = kvn[h].astype(F32).T.astype(BF16)
    for d, q in enumerate((q0, q1, q2, q3)):
        qd[d] = q[...]

    freq = frequency((16, TOK), 0)
    for p in range(4):
        place = qd[p, pl.ds(2 * GROUP, 16), :].astype(F32)
        for k, table in enumerate(sub_tables(place[0:1], place[1:2], freq)):
            tables[p, pl.ds(16 * k, 16), :] = table

    def step(h, carry):
        at = pl.ds(pl.multiple_of(64 * h, 64), 64)
        kv = kvn[h]
        kv_t = kvt[h]
        total = None
        outs = []
        for p in range(4):
            q = qd[p, at, :]
            do = qd[p, pl.ds(pl.multiple_of(GROUP + 64 * h, 64), 64), :]
            zero = jnp.zeros_like(q)
            q_pad = jnp.concatenate([q, zero], axis=0)
            do_pad = jnp.concatenate([zero, do], axis=0)
            scores = mm(kv, q_pad)
            top = jnp.max(scores, axis=0, keepdims=True)
            expo = jnp.exp(scores - top)
            denom = jnp.sum(expo, axis=0, keepdims=True)
            inv = 1.0 / denom
            mixed = mm(kv_t[64:128], expo.astype(BF16)) * inv
            mixed = mixed.astype(BF16)
            delta = jnp.sum(mixed.astype(F32) * do.astype(F32), axis=0, keepdims=True)
            prob = expo * inv
            dprob = mm(kv, do_pad)
            dscore = (prob * (dprob - delta)).astype(BF16)
            dq = mm(kv_t[0:64], dscore) * 0.125
            table = [tables[p, pl.ds(16 * k, 16), :] for k in range(4)]
            outs.append((mixed, sub_turn(dq, table, -1.0).astype(BF16)))
            part = mm(dscore, q_pad, ((1,), (1,))) + mm(prob.astype(BF16), do_pad, ((1,), (1,)))
            total = part if total is None else total + part
        for p, (mixed, dq) in enumerate(outs):
            att[p, at, :] = mixed
            dq_ref[(x + 4 - p) % 4, at, :] = dq
        keep_ref[h] = total[0:512]
        send_ref[h] = total[512:1024].astype(BF16)
        return carry

    lax.fori_loop(0, 3, step, 0)
    for d, a in enumerate((a0, a1, a2, a3)):
        a[...] = att[d]


def attention(xs, qs, us):
    out = jax.ShapeDtypeStruct((GROUP, TOK), BF16)
    return pl.pallas_call(
        attention_kernel,
        in_specs=[smem()] + [vmem()] * 8,
        out_specs=[vmem()] * 7,
        out_shape=[out] * 4
        + [
            jax.ShapeDtypeStruct((4, GROUP, TOK), BF16),
            jax.ShapeDtypeStruct((3, 512, 128), F32),
            jax.ShapeDtypeStruct((3, 512, 128), BF16),
        ],
        scratch_shapes=[
            pltpu.VMEM((3, 1024, 128), BF16),
            pltpu.VMEM((3, 128, 1024), BF16),
            pltpu.VMEM((4, MSG, TOK), BF16),
            pltpu.VMEM((4, GROUP, TOK), BF16),
            pltpu.VMEM((4, 64, TOK), F32),
        ],
        compiler_params=params(56),
        cost_estimate=cost(20),
        name="attention",
    )(xs, *qs, *us)


def table_kernel(q0, q1, q2, q3, cos_ref, sin_ref):
    freq = frequency((1, 128), 1)
    i = lax.broadcasted_iota(jnp.int32, (32, 128), 0).astype(F32)
    left = lax.broadcasted_iota(jnp.int32, (32, 128), 1) < 64
    for d, q in enumerate((q0, q1, q2, q3)):
        place = q[pl.ds(2 * GROUP, 16), :].astype(F32)
        for b in range(2):
            row = jnp.broadcast_to(place[0:1, 128 * b : 128 * b + 1], (32, 128)) + 0.5
            col = jnp.broadcast_to(place[1:2, 128 * b : 128 * b + 1], (32, 128)) + 0.5 + 2.0 * i
            cos, sin, even = lane_tables(row * freq, col * freq, -1.0)
            at = pl.ds(64 * d + 32 * b, 32)
            cos_ref[at, :] = jnp.where(left, cos, 1.0)
            sin_ref[at, :] = jnp.where(left, sin, 0.0)


def key_tables(qs):
    out = jax.ShapeDtypeStruct((TOK, 128), F32)
    return pl.pallas_call(
        table_kernel,
        in_specs=[vmem()] * 4,
        out_specs=[vmem()] * 2,
        out_shape=[out] * 2,
        compiler_params=params(56),
        cost_estimate=cost(2),
        name="key_tables",
    )(*qs)


def dkv_kernel(x_ref, cos_ref, sin_ref, keep_ref, core_ref, y_ref, out_ref):
    x = x_ref[0]
    even = (lax.broadcasted_iota(jnp.int32, (CELLS, 128), 1) & 31) < 16
    for d in range(4):
        at = pl.ds(64 * d, 64)
        for h in range(3):
            total = keep_ref[h, at, :] + core_ref[h, at, :].astype(F32) + y_ref[h, at, :].astype(F32)
            out_ref[(x + 4 - d) % 4, h] = turn(total, cos_ref[at, :], sin_ref[at, :], even).astype(BF16)


def finish_dkv(xs, tables, keep, core, y):
    half = pl.BlockSpec((3, 256, 128), lambda i: (0, 0, 0))
    return pl.pallas_call(
        dkv_kernel,
        grid=(1,),
        in_specs=[smem(), pl.BlockSpec((TOK, 128), lambda i: (0, 0)), pl.BlockSpec((TOK, 128), lambda i: (0, 0)), half, half, half],
        out_specs=pl.BlockSpec((4, 3, CELLS, 128), lambda i: (0, 0, 0, 0)),
        out_shape=jax.ShapeDtypeStruct((4, 3, CELLS, 128), BF16),
        compiler_params=params(56),
        cost_estimate=cost(2),
        name="finish_dkv",
    )(xs, *tables, keep, core, y)


def term_q_kernel(x_ref, c_ref, t0, t1, t2, t3, d0, d1, d2, d3, wm_ref, keep_ref, send_ref, tokf, merged_ref, scr, rows):
    x = x_ref[0]
    toks = (t0, t1, t2, t3)
    for d, t in enumerate(toks):
        for k in range(3):
            tokf[k, pl.ds(256 * d, 256), :] = t[:, pl.ds(128 * k, 128)].astype(F32)
    merged_ref[...] = jnp.concatenate([merge(tokf, wm_ref, k, 256) for k in range(3)], axis=1).astype(BF16)
    for e, dq in enumerate((d0, d1, d2, d3)):
        total = None
        for d in range(4):
            one = mm(dq[(x + 4 - d) % 4], toks[d][...])
            total = one if total is None else total + one
        scr[(x + 4 - e) % 4] = total
    full = jnp.concatenate([scr[0], scr[1], scr[2], scr[3]], axis=0).T
    for r in range(4):
        rows[r] = full[96 * r : 96 * r + 96]
    c = c_ref[0]
    for h in range(2):
        keep_ref[h] = rows[2 * h + c]
        send_ref[h] = rows[2 * h + 1 - c].astype(BF16)


def term_q(xs, cs, toks, dqs, w_merge):
    return pl.pallas_call(
        term_q_kernel,
        in_specs=[smem()] * 2 + [vmem()] * 9,
        out_specs=[vmem()] * 4,
        out_shape=[
            jax.ShapeDtypeStruct((2, 96, HD), F32),
            jax.ShapeDtypeStruct((2, 96, HD), BF16),
            jax.ShapeDtypeStruct((3, 1024, 128), F32),
            jax.ShapeDtypeStruct((TOK, ROWS), BF16),
        ],
        scratch_shapes=[pltpu.VMEM((4, GROUP, ROWS), F32), pltpu.VMEM((4, 96, HD), F32)],
        compiler_params=params(12),
        cost_estimate=cost(4),
        name="term_q",
    )(xs, cs, *toks, *dqs, w_merge)


def natural(tiles, rows, put):
    left = lax.broadcasted_iota(jnp.int32, (rows, 128), 1) < 64
    for k in range(6):
        a = tiles(2 * k).astype(F32)
        b = tiles(2 * k + 1).astype(F32)
        put(128 * k, jnp.where(left, a, pltpu.roll(b, 64, 1)).astype(BF16))
        put(HD + 128 * k, jnp.where(left, pltpu.roll(a, 64, 1), b).astype(BF16))


def term_kv_kernel(x_ref, c_ref, tokf, merged_ref, k0, k1, k2, k3, wkv_ref, keep_ref, send_ref, tiles, dkv, full, m_ref):
    x = x_ref[0]
    c = c_ref[0]
    for e, k in enumerate((k0, k1, k2, k3)):
        group = (x + 4 - e) % 4
        for d in range(4):
            for h in range(3):
                tiles[group * 3 + h, pl.ds(64 * d, 64), :] = k[(x + 4 - d) % 4, h]

    def put(at, value):
        dkv[:, pl.ds(at, 128)] = value

    natural(lambda h: tiles[h], 256, put)
    grad = dkv[...]
    term = mm(merged_ref[...], grad, ((0,), (0,)))
    for r in range(4):
        full[r, :, pl.ds(0, D)] = term[96 * r : 96 * r + 96]
    dmerged = mm(grad, wkv_ref[...], ((1,), (1,)))
    for t in range(4):
        for k in range(3):
            one = dmerged[:, 128 * k : 128 * k + 128] * tokf[k, pl.ds(t, 256, stride=4), :]
            m_ref[t : t + 1, pl.ds(128 * k, 128)] = jnp.sum(one, axis=0, keepdims=True)
    m_ref[4:8, :] = jnp.zeros((4, ROWS), F32)
    m = m_ref[...]
    for r in range(4):
        full[r, :, pl.ds(D, 128)] = jnp.zeros((96, 128), F32)
        full[r, pl.ds(0, 8), pl.ds(D, 128)] = jnp.concatenate([m[:, 96 * r : 96 * r + 96], jnp.zeros((8, 32), F32)], axis=1)
    for h in range(2):
        keep_ref[h] = full[2 * h + c]
        send_ref[h] = full[2 * h + 1 - c].astype(BF16)


def term_kv(xs, cs, tokf, merged, dkvs, w_kv):
    spec = lambda shape: pl.BlockSpec(shape, lambda i, x, c: (0,) * len(shape))
    grid_spec = pltpu.PrefetchScalarGridSpec(
        num_scalar_prefetch=2,
        grid=(1,),
        in_specs=[spec((3, 1024, 128)), spec((TOK, ROWS))]
        + [spec((4, 3, CELLS, 128))] * 4
        + [spec((ROWS, D))],
        out_specs=[spec((2, 96, D + 128)), spec((2, 96, D + 128))],
        scratch_shapes=[
            pltpu.VMEM((12, 256, 128), BF16),
            pltpu.VMEM((256, D), BF16),
            pltpu.VMEM((4, 96, D + 128), F32),
            pltpu.VMEM((8, ROWS), F32),
        ],
    )
    return pl.pallas_call(
        term_kv_kernel,
        grid_spec=grid_spec,
        out_shape=[
            jax.ShapeDtypeStruct((2, 96, D + 128), F32),
            jax.ShapeDtypeStruct((2, 96, D + 128), BF16),
        ],
        compiler_params=params(11),
        cost_estimate=cost(5),
        name="term_kv",
    )(xs, cs, tokf, merged, *dkvs, w_kv)


def grad_tokens_kernel(x_ref, d0, d1, d2, d3, k0, k1, k2, k3, wq_ref, wkv_ref, wm_ref, out_ref, tiles, dkv, dqs, back):
    x = x_ref[0]
    for e, (q, k) in enumerate(((d0, k0), (d1, k1), (d2, k2), (d3, k3))):
        group = (x + 4 - e) % 4
        dqs[group] = q[0]
        for h in range(3):
            tiles[group * 3 + h] = k[0, h]

    def put(at, value):
        dkv[:, pl.ds(at, 128)] = value

    natural(lambda h: tiles[h], CELLS, put)
    dq = jnp.concatenate([dqs[g].astype(F32).T.astype(BF16) for g in range(4)], axis=1)
    full = mm(dq, wq_ref[...], ((1,), (1,)))
    dmerged = mm(dkv[...], wkv_ref[...], ((1,), (1,)))
    for k in range(12):
        lanes = pl.ds(128 * k, 128)
        back[k] = full[:, 128 * k : 128 * k + 128]
        for t in range(4):
            at = pl.ds(t, CELLS, stride=4)
            back[k, at, :] = back[k, at, :] + wm_ref[t : t + 1, lanes] * dmerged[:, 128 * k : 128 * k + 128]
        out_ref[0, :, lanes] = back[k].astype(BF16)


def grad_of_tokens(xs, dqs, dkvs, w_query, w_kv, w_merge):
    spec = lambda shape: pl.BlockSpec(shape, lambda i, x: (0,) * len(shape))
    grid_spec = pltpu.PrefetchScalarGridSpec(
        num_scalar_prefetch=1,
        grid=(1,),
        in_specs=[pl.BlockSpec((1, GROUP, TOK), lambda i, x: (x[0], 0, 0))] * 4
        + [pl.BlockSpec((1, 3, CELLS, 128), lambda i, x: (x[0], 0, 0, 0))] * 4
        + [spec((D, HD)), spec((D, D)), spec((4, D))],
        out_specs=spec((1, TOK, D)),
        scratch_shapes=[
            pltpu.VMEM((12, CELLS, 128), BF16),
            pltpu.VMEM((CELLS, D), BF16),
            pltpu.VMEM((4, GROUP, TOK), BF16),
            pltpu.VMEM((12, TOK, 128), F32),
        ],
    )
    return pl.pallas_call(
        grad_tokens_kernel,
        grid_spec=grid_spec,
        out_shape=jax.ShapeDtypeStruct((1, TOK, D), BF16),
        compiler_params=params(56),
        cost_estimate=cost(6),
        name="grad_tokens",
    )(xs, *dqs, *dkvs, w_query, w_kv, w_merge)


def spread_x(parts):
    return [parts[0]] + [lax.ppermute(parts[k], "seq", X_SHIFT[k]) for k in range(1, 4)]


def after(value, earlier):
    return lax.optimization_barrier((value, earlier))[0]


def core_sum(keep, send, y):
    got = lax.ppermute(send, "seq", CORE_SWAP)
    summed = keep + got.astype(F32)
    mine = lax.dynamic_index_in_dim(summed, y, 0, False)
    theirs = lax.dynamic_index_in_dim(summed, 1 - y, 0, False).astype(BF16)
    return mine, theirs


def on_device(tokens, keep_index, d_out, w_query, w_kv, w_merge):
    own = tokens[0]
    place = lax.axis_index("seq")
    x = place // 4
    y = (place // 2) % 2
    c = place % 2
    xs = x.reshape(1)
    cs = c.reshape(1)
    parts = keyval(xs, keep_index[0], own, w_merge, w_kv)
    got_kv = spread_x(parts)
    q_parts = queries(xs, keep_index, own, w_query, d_out[0])
    got_kv, q_parts = lax.optimization_barrier((got_kv, q_parts))
    unit = jnp.stack(got_kv)
    qs = spread_x(q_parts)
    unit_c = lax.ppermute(unit, "seq", CORE_SWAP)
    unit_y = lax.ppermute(unit, "seq", Y_SWAP)
    unit_cy = lax.ppermute(unit_y, "seq", CORE_SWAP)

    held = after(own, qs[1])
    slices = [lax.dynamic_slice(held, (0, ROWS * ((x + k) % 4)), (TOK, ROWS)) for k in range(4)]
    toks = spread_x(slices)

    a0, a1, a2, a3, dq, keep, send = attention(xs, qs, [unit, unit_y, unit_c, unit_cy])
    dq, keep, send, toks = lax.optimization_barrier((dq, keep, send, toks))
    dqs = [dq] + [lax.ppermute(dq, "seq", X_SHIFT[k]) for k in range(1, 4)]
    core = lax.ppermute(send, "seq", CORE_SWAP)
    other = (keep[:, 256:] + core[:, 256:].astype(F32)).astype(BF16)
    from_y = lax.ppermute(other, "seq", Y_SWAP)
    taps, weights = after((w_merge, w_kv), other)
    taps = lax.dynamic_slice(taps, (0, ROWS * x), (4, ROWS))
    weights = lax.dynamic_slice(weights, (ROWS * x, 0), (ROWS, D))
    tables = key_tables(after(qs, other))
    dkv = finish_dkv(xs, tables, keep, core, from_y)
    dkvs = [dkv] + [lax.ppermute(dkv, "seq", X_SHIFT[k]) for k in range(1, 4)]

    keep_q, send_q, tokf, unit_merged = term_q(xs, cs, toks, after(dqs, dkv), taps)
    keep_kv, send_kv = term_kv(xs, cs, tokf, unit_merged, dkvs, weights)
    mine_q, theirs_q = core_sum(keep_q, after(send_q, dkv), y)

    mine, theirs = core_sum(keep_kv, send_kv, y)
    theirs_q = after(theirs_q, theirs)
    got_q = lax.ppermute(theirs_q, "seq", Y_SWAP)
    got = lax.ppermute(theirs, "seq", Y_SWAP)
    grads = grad_of_tokens(xs, after(dqs, (theirs, theirs_q)), dkvs, w_query, w_kv, w_merge)
    got, got_q = after((got, got_q), grads)
    total = mine + got.astype(F32)
    total = total.astype(BF16)
    m = jnp.broadcast_to(total[None, :24, D:], (8, 24, 128))
    total = total[:, :D].reshape(4, 24, 2, 768).transpose(0, 2, 1, 3).reshape(8, 24, 768)
    total_q = (mine_q + got_q.astype(F32)).astype(BF16)
    total_q = total_q.reshape(4, 24, 2, 384).transpose(0, 2, 1, 3).reshape(8, 24, 384)
    chunks = jnp.concatenate([total_q, total, m], axis=2)
    shards = lax.all_to_all(chunks, "dp", 0, 0, axis_index_groups=Z_GROUPS)
    a1, a2, a3 = after((a1, a2, a3), chunks)
    back = [a0] + [lax.ppermute(a, "seq", X_SHIFT[4 - k]) for k, a in ((1, a1), (2, a2), (3, a3))]
    order = jnp.stack(back)
    att = jnp.concatenate([lax.dynamic_index_in_dim(order, (g + 4 - x) % 4, 0, False) for g in range(4)], axis=0)
    attended = att.T

    shard = jnp.sum(shards.astype(F32), axis=0).astype(BF16)
    pair = lax.ppermute(shard, "dp", YLO_SWAP)
    shard = shard.astype(F32) + pair.astype(F32)
    grad_m = shard[:4, 1152 : 1152 + 96]
    final = shard[:, :1152].astype(BF16)
    final = lax.all_to_all(jnp.broadcast_to(final[None], (8, 24, 1152)), "dp", 0, 0, axis_index_groups=Z_GROUPS)
    final = final.reshape(4, 2, 24, 1152).transpose(0, 2, 1, 3)
    grad_q = final[..., :384].reshape(96, HD).astype(F32)
    grad_kv = final[..., 384:].reshape(96, D).astype(F32)
    return attended[None], grads, grad_q, grad_kv, grad_m


def solution(mesh):
    placed = (P("dp", "seq", None), P("dp", "seq"), P("dp", "seq", None), P(), P(), P())
    return jax.shard_map(
        on_device,
        mesh=mesh,
        in_specs=placed,
        out_specs=(
            P("dp", "seq", None),
            P("dp", "seq", None),
            P("seq", None),
            P("seq", None),
            P(None, "seq"),
        ),
        check_vma=False,
    )
```

```python
import jax
import jax.numpy as jnp
import numpy as np
from jax import lax
from jax.experimental import pallas as pl
from jax.experimental.pallas import tpu as pltpu
from jax.sharding import PartitionSpec as P

D = 1536
HD = 768
HEADS = 12
HEAD = 64
GROUP = 192
ROWS = 384
TOK = 256
CELLS = 64
MSG = 400
FREQ = (100.0 ** (-np.arange(16, dtype=np.float64) / 16)).astype(np.float32)
F32 = jnp.float32
BF16 = jnp.bfloat16

X_SHIFT = [[(i, (((i >> 2) + k) % 4) * 4 + (i & 3)) for i in range(16)] for k in range(4)]
Y_SWAP = [(i, i ^ 2) for i in range(16)]
CORE_SWAP = [(i, i ^ 1) for i in range(16)]
YLO_SWAP = [(i, i ^ 8) for i in range(16)]
Z_GROUPS = [list(range(8)), list(range(8, 16))]


def params(mib):
    return pltpu.CompilerParams(vmem_limit_bytes=mib * 1024 * 1024)


def cost(us):
    return pl.CostEstimate(flops=int(us * 1.1e9), bytes_accessed=int(us * 1e5), transcendentals=0)


def vmem():
    return pl.BlockSpec(memory_space=pltpu.VMEM)


def smem():
    return pl.BlockSpec(memory_space=pltpu.SMEM)


def mm(a, b, dims=((1,), (0,))):
    return lax.dot_general(a, b, (dims, ((), ())), preferred_element_type=F32)


def frequency(shape, axis):
    j = lax.broadcasted_iota(jnp.int32, shape, axis) & 15
    freq = jnp.zeros(shape, F32)
    for k in range(16):
        freq = jnp.where(j == k, float(FREQ[k]), freq)
    return freq


def hbm():
    return pl.BlockSpec(memory_space=pltpu.MemorySpace.HBM)


def lane_tables(row, col, sign):
    lane = lax.broadcasted_iota(jnp.int32, row.shape, 1)
    angle = jnp.where((lane & 63) < 32, row, col)
    even = (lane & 31) < 16
    return jnp.cos(angle), jnp.sin(angle) * jnp.where(even, -sign, sign), even


def turn(u, cos, sin, even):
    swapped = jnp.where(even, pltpu.roll(u, 112, 1), pltpu.roll(u, 16, 1))
    return u * cos + swapped * sin


def merge(tokf, wm_ref, k, cells):
    total = None
    for t in range(4):
        one = tokf[k, pl.ds(t, cells, stride=4), :] * wm_ref[t : t + 1, pl.ds(128 * k, 128)]
        total = one if total is None else total + one
    return total


def keyval_kernel(x_ref, idx_ref, tok_hbm, wm_hbm, wkv_ref, o0, o1, o2, o3, tok_ref, wm_ref, tokf, merged, weights, piece, sems):
    copies = [pltpu.make_async_copy(wkv_ref.at[:, pl.ds(512 * j, 512)], weights.at[j], sems.at[j]) for j in range(3)]
    first = [pltpu.make_async_copy(tok_hbm, tok_ref, sems.at[3]), pltpu.make_async_copy(wm_hbm, wm_ref, sems.at[4])]
    for one in first + copies:
        one.start()
    freq = frequency((1, 128), 1)
    i = lax.broadcasted_iota(jnp.int32, (CELLS, 128), 0)
    start = idx_ref[0] // 4
    second = idx_ref[128] // 4
    cell = jnp.where(i < 32, start + i, second + i - 32)
    row = (2 * (cell >> 6)).astype(F32) + 0.5
    col = (2 * (cell & 63)).astype(F32) + 0.5
    cos, sin, even = lane_tables(row * freq, col * freq, 1.0)
    left = lax.broadcasted_iota(jnp.int32, (CELLS, 128), 1) < 64
    for one in first:
        one.wait()
    for k in range(12):
        tokf[k] = tok_ref[:, pl.ds(128 * k, 128)].astype(F32)
        merged[:, pl.ds(128 * k, 128)] = merge(tokf, wm_ref, k, CELLS).astype(BF16)
    tiles = []
    for j in range(3):
        copies[j].wait()
        part = mm(merged[...], weights[j])
        tiles += [part[:, 128 * k : 128 * k + 128] for k in range(4)]
    for k in range(6):
        key = turn(tiles[k], cos, sin, even)
        val = tiles[6 + k]
        a = jnp.where(left, key, pltpu.roll(val, 64, 1)).astype(BF16)
        b = jnp.where(left, pltpu.roll(key, 64, 1), val).astype(BF16)
        piece[(2 * k) // 3, (2 * k) % 3] = a
        piece[(2 * k + 1) // 3, (2 * k + 1) % 3] = b
    x = x_ref[0]
    for d, out in enumerate((o0, o1, o2, o3)):
        out[...] = piece[(x + d) % 4]


def keyval(xs, index, tokens, w_merge, w_kv):
    out = jax.ShapeDtypeStruct((3, CELLS, 128), BF16)
    return pl.pallas_call(
        keyval_kernel,
        in_specs=[smem(), smem(), hbm(), hbm(), hbm()],
        out_specs=[vmem()] * 4,
        out_shape=[out] * 4,
        scratch_shapes=[
            pltpu.VMEM((TOK, D), BF16),
            pltpu.VMEM((4, D), F32),
            pltpu.VMEM((12, TOK, 128), F32),
            pltpu.VMEM((CELLS, D), BF16),
            pltpu.VMEM((3, D, 512), BF16),
            pltpu.VMEM((4, 3, CELLS, 128), BF16),
            pltpu.SemaphoreType.DMA((5,)),
        ],
        compiler_params=params(56),
        cost_estimate=cost(6),
        name="keyval",
    )(xs, index, tokens, w_merge, w_kv)


def sub_tables(row, col, freq):
    return (
        jnp.cos(row * freq),
        jnp.sin(row * freq),
        jnp.cos(col * freq),
        jnp.sin(col * freq),
    )


def sub_turn(u, tables, sign):
    rc, rs, cc, cs = tables
    a, b, c, d = u[0:16], u[16:32], u[32:48], u[48:64]
    return jnp.concatenate(
        [
            a * rc - sign * (b * rs),
            sign * (a * rs) + b * rc,
            c * cc - sign * (d * cs),
            sign * (c * cs) + d * cc,
        ],
        axis=0,
    )


def query_kernel(x_ref, idx_ref, tok_ref, wq_ref, do_ref, o0, o1, o2, o3, scr):
    index = idx_ref[...]
    cell = index >> 2
    row = 2 * (cell >> 6) + ((index >> 1) & 1)
    col = 2 * (cell & 63) + (index & 1)
    row = row.astype(F32)
    col = col.astype(F32)
    tables = sub_tables(row, col, frequency((16, TOK), 0))
    query = mm(tok_ref[...], wq_ref[...]).T
    same = lax.broadcasted_iota(jnp.int32, (TOK, TOK), 0) == lax.broadcasted_iota(jnp.int32, (TOK, TOK), 1)
    same = jnp.where(same, 1.0, 0.0).astype(BF16)
    grad = [mm(same, do_ref[:, pl.ds(256 * k, 256)], ((1,), (1,))).astype(BF16) for k in range(3)]
    grad = jnp.concatenate(grad, axis=0)
    line = lax.broadcasted_iota(jnp.int32, (16, TOK), 0)
    place = jnp.where(line == 0, row, jnp.where(line == 1, col, 0.0)).astype(BF16)
    for h in range(HEADS):
        g, k = h // 3, h % 3
        scr[g, pl.ds(64 * k, 64), :] = (sub_turn(query[64 * h : 64 * h + 64], tables, 1.0) * 0.125).astype(BF16)
    for g in range(4):
        scr[g, pl.ds(GROUP, GROUP), :] = grad[GROUP * g : GROUP * g + GROUP]
        scr[g, pl.ds(2 * GROUP, 16), :] = place
    x = x_ref[0]
    for d, out in enumerate((o0, o1, o2, o3)):
        out[...] = scr[(x + d) % 4]


def queries(xs, index, tokens, w_query, grad):
    out = jax.ShapeDtypeStruct((MSG, TOK), BF16)
    return pl.pallas_call(
        query_kernel,
        in_specs=[smem()] + [vmem()] * 4,
        out_specs=[vmem()] * 4,
        out_shape=[out] * 4,
        scratch_shapes=[pltpu.VMEM((4, MSG, TOK), BF16)],
        compiler_params=params(8),
        cost_estimate=cost(4),
        name="queries",
    )(xs, index, tokens, w_query, grad)


def attention_kernel(
    x_ref, q0, q1, q2, q3, u0, u1, u2, u3, a0, a1, a2, a3, dq_ref, keep_ref, send_ref, kvn, kvt, qd, att, tables, pairs
):
    x = x_ref[0]
    for k, u in enumerate((u0, u1, u2, u3)):
        for d in range(4):
            for h in range(3):
                kvn[h, pl.ds(256 * k + 64 * d, 64), :] = u[d, h]
    for h in range(3):
        kvt[h] = kvn[h].astype(F32).T.astype(BF16)
    for d, q in enumerate((q0, q1, q2, q3)):
        qd[d] = q[...]

    freq = frequency((16, TOK), 0)
    for p in range(4):
        place = qd[p, pl.ds(2 * GROUP, 16), :].astype(F32)
        for k, table in enumerate(sub_tables(place[0:1], place[1:2], freq)):
            tables[p, pl.ds(16 * k, 16), :] = table

    def step(i, carry):
        total = None
        outs = []
        for j in range(6):
            h = (6 * i + j) // 4
            p = (6 * i + j) % 4
            at = pl.ds(pl.multiple_of(64 * h, 64), 64)
            kv = kvn[h]
            kv_t = kvt[h]
            q = qd[p, at, :]
            do = qd[p, pl.ds(pl.multiple_of(GROUP + 64 * h, 64), 64), :]
            zero = jnp.zeros_like(q)
            q_pad = jnp.concatenate([q, zero], axis=0)
            do_pad = jnp.concatenate([zero, do], axis=0)
            scores = mm(kv, q_pad)
            top = jnp.max(scores, axis=0, keepdims=True)
            expo = jnp.exp(scores - top)
            denom = jnp.sum(expo, axis=0, keepdims=True)
            inv = 1.0 / denom
            mixed = mm(kv_t[64:128], expo.astype(BF16)) * inv
            mixed = mixed.astype(BF16)
            delta = jnp.sum(mixed.astype(F32) * do.astype(F32), axis=0, keepdims=True)
            prob = expo * inv
            dprob = mm(kv, do_pad)
            dscore = (prob * (dprob - delta)).astype(BF16)
            dq = mm(kv_t[0:64], dscore) * 0.125
            table = [tables[p, pl.ds(16 * k, 16), :] for k in range(4)]
            outs.append((p, at, mixed, sub_turn(dq, table, -1.0).astype(BF16)))
            part = mm(dscore, q_pad, ((1,), (1,))) + mm(prob.astype(BF16), do_pad, ((1,), (1,)))
            total = part if j % 2 == 0 else total + part
            if j % 2 == 1:
                pairs[3 * i + j // 2] = total
        for p, at, mixed, dq in outs:
            att[p, at, :] = mixed
            dq_ref[(x + 4 - p) % 4, at, :] = dq
        return carry

    lax.fori_loop(0, 2, step, 0)
    for h in range(3):
        total = pairs[2 * h] + pairs[2 * h + 1]
        keep_ref[h] = total[0:512]
        send_ref[h] = total[512:1024].astype(BF16)
    for d, a in enumerate((a0, a1, a2, a3)):
        a[...] = att[d]


def attention(xs, qs, us):
    out = jax.ShapeDtypeStruct((GROUP, TOK), BF16)
    return pl.pallas_call(
        attention_kernel,
        in_specs=[smem()] + [vmem()] * 8,
        out_specs=[vmem()] * 7,
        out_shape=[out] * 4
        + [
            jax.ShapeDtypeStruct((4, GROUP, TOK), BF16),
            jax.ShapeDtypeStruct((3, 512, 128), F32),
            jax.ShapeDtypeStruct((3, 512, 128), BF16),
        ],
        scratch_shapes=[
            pltpu.VMEM((3, 1024, 128), BF16),
            pltpu.VMEM((3, 128, 1024), BF16),
            pltpu.VMEM((4, MSG, TOK), BF16),
            pltpu.VMEM((4, GROUP, TOK), BF16),
            pltpu.VMEM((4, 64, TOK), F32),
            pltpu.VMEM((6, 1024, 128), F32),
        ],
        compiler_params=params(56),
        cost_estimate=cost(20),
        name="attention",
    )(xs, *qs, *us)


def table_kernel(q0, q1, q2, q3, cos_ref, sin_ref):
    freq = frequency((1, 128), 1)
    i = lax.broadcasted_iota(jnp.int32, (32, 128), 0).astype(F32)
    left = lax.broadcasted_iota(jnp.int32, (32, 128), 1) < 64
    for d, q in enumerate((q0, q1, q2, q3)):
        place = q[pl.ds(2 * GROUP, 16), :].astype(F32)
        for b in range(2):
            row = jnp.broadcast_to(place[0:1, 128 * b : 128 * b + 1], (32, 128)) + 0.5
            col = jnp.broadcast_to(place[1:2, 128 * b : 128 * b + 1], (32, 128)) + 0.5 + 2.0 * i
            cos, sin, even = lane_tables(row * freq, col * freq, -1.0)
            at = pl.ds(64 * d + 32 * b, 32)
            cos_ref[at, :] = jnp.where(left, cos, 1.0)
            sin_ref[at, :] = jnp.where(left, sin, 0.0)


def key_tables(qs):
    out = jax.ShapeDtypeStruct((TOK, 128), F32)
    return pl.pallas_call(
        table_kernel,
        in_specs=[vmem()] * 4,
        out_specs=[vmem()] * 2,
        out_shape=[out] * 2,
        compiler_params=params(56),
        cost_estimate=cost(2),
        name="key_tables",
    )(*qs)


def dkv_kernel(x_ref, cos_ref, sin_ref, keep_ref, core_ref, y_ref, out_ref):
    x = x_ref[0]
    even = (lax.broadcasted_iota(jnp.int32, (CELLS, 128), 1) & 31) < 16
    for d in range(4):
        at = pl.ds(64 * d, 64)
        for h in range(3):
            total = keep_ref[h, at, :] + core_ref[h, at, :].astype(F32) + y_ref[h, at, :].astype(F32)
            out_ref[(x + 4 - d) % 4, h] = turn(total, cos_ref[at, :], sin_ref[at, :], even).astype(BF16)


def finish_dkv(xs, tables, keep, core, y):
    half = pl.BlockSpec((3, 256, 128), lambda i: (0, 0, 0))
    return pl.pallas_call(
        dkv_kernel,
        grid=(1,),
        in_specs=[smem(), pl.BlockSpec((TOK, 128), lambda i: (0, 0)), pl.BlockSpec((TOK, 128), lambda i: (0, 0)), half, half, half],
        out_specs=pl.BlockSpec((4, 3, CELLS, 128), lambda i: (0, 0, 0, 0)),
        out_shape=jax.ShapeDtypeStruct((4, 3, CELLS, 128), BF16),
        compiler_params=params(56),
        cost_estimate=cost(2),
        name="finish_dkv",
    )(xs, *tables, keep, core, y)


def term_q_kernel(x_ref, c_ref, t0, t1, t2, t3, d0, d1, d2, d3, wm_ref, keep_ref, send_ref, tokf, merged_ref, scr, rows):
    x = x_ref[0]
    toks = (t0, t1, t2, t3)
    for d, t in enumerate(toks):
        for k in range(3):
            tokf[k, pl.ds(256 * d, 256), :] = t[:, pl.ds(128 * k, 128)].astype(F32)
    merged_ref[...] = jnp.concatenate([merge(tokf, wm_ref, k, 256) for k in range(3)], axis=1).astype(BF16)
    for e, dq in enumerate((d0, d1, d2, d3)):
        total = None
        for d in range(4):
            one = mm(dq[(x + 4 - d) % 4], toks[d][...])
            total = one if total is None else total + one
        scr[(x + 4 - e) % 4] = total
    full = jnp.concatenate([scr[0], scr[1], scr[2], scr[3]], axis=0).T
    for r in range(4):
        rows[r] = full[96 * r : 96 * r + 96]
    c = c_ref[0]
    for h in range(2):
        keep_ref[h] = rows[2 * h + c]
        send_ref[h] = rows[2 * h + 1 - c].astype(BF16)


def term_q(xs, cs, toks, dqs, w_merge):
    return pl.pallas_call(
        term_q_kernel,
        in_specs=[smem()] * 2 + [vmem()] * 9,
        out_specs=[vmem()] * 4,
        out_shape=[
            jax.ShapeDtypeStruct((2, 96, HD), F32),
            jax.ShapeDtypeStruct((2, 96, HD), BF16),
            jax.ShapeDtypeStruct((3, 1024, 128), F32),
            jax.ShapeDtypeStruct((TOK, ROWS), BF16),
        ],
        scratch_shapes=[pltpu.VMEM((4, GROUP, ROWS), F32), pltpu.VMEM((4, 96, HD), F32)],
        compiler_params=params(12),
        cost_estimate=cost(4),
        name="term_q",
    )(xs, cs, *toks, *dqs, w_merge)


def natural(tiles, rows, put):
    left = lax.broadcasted_iota(jnp.int32, (rows, 128), 1) < 64
    for k in range(6):
        a = tiles(2 * k).astype(F32)
        b = tiles(2 * k + 1).astype(F32)
        put(128 * k, jnp.where(left, a, pltpu.roll(b, 64, 1)).astype(BF16))
        put(HD + 128 * k, jnp.where(left, pltpu.roll(a, 64, 1), b).astype(BF16))


def term_kv_kernel(x_ref, c_ref, tokf, merged_ref, k0, k1, k2, k3, wkv_ref, keep_ref, send_ref, tiles, dkv, full, m_ref):
    x = x_ref[0]
    c = c_ref[0]
    for e, k in enumerate((k0, k1, k2, k3)):
        group = (x + 4 - e) % 4
        for d in range(4):
            for h in range(3):
                tiles[group * 3 + h, pl.ds(64 * d, 64), :] = k[(x + 4 - d) % 4, h]

    def put(at, value):
        dkv[:, pl.ds(at, 128)] = value

    natural(lambda h: tiles[h], 256, put)
    grad = dkv[...]
    term = mm(merged_ref[...], grad, ((0,), (0,)))
    for r in range(4):
        full[r, :, pl.ds(0, D)] = term[96 * r : 96 * r + 96]
    dmerged = mm(grad, wkv_ref[...], ((1,), (1,)))
    for t in range(4):
        for k in range(3):
            one = dmerged[:, 128 * k : 128 * k + 128] * tokf[k, pl.ds(t, 256, stride=4), :]
            m_ref[t : t + 1, pl.ds(128 * k, 128)] = jnp.sum(one, axis=0, keepdims=True)
    m_ref[4:8, :] = jnp.zeros((4, ROWS), F32)
    m = m_ref[...]
    for r in range(4):
        full[r, :, pl.ds(D, 128)] = jnp.zeros((96, 128), F32)
        full[r, pl.ds(0, 8), pl.ds(D, 128)] = jnp.concatenate([m[:, 96 * r : 96 * r + 96], jnp.zeros((8, 32), F32)], axis=1)
    for h in range(2):
        keep_ref[h] = full[2 * h + c]
        send_ref[h] = full[2 * h + 1 - c].astype(BF16)


def term_kv(xs, cs, tokf, merged, dkvs, w_kv):
    spec = lambda shape: pl.BlockSpec(shape, lambda i, x, c: (0,) * len(shape))
    grid_spec = pltpu.PrefetchScalarGridSpec(
        num_scalar_prefetch=2,
        grid=(1,),
        in_specs=[spec((3, 1024, 128)), spec((TOK, ROWS))]
        + [spec((4, 3, CELLS, 128))] * 4
        + [spec((ROWS, D))],
        out_specs=[spec((2, 96, D + 128)), spec((2, 96, D + 128))],
        scratch_shapes=[
            pltpu.VMEM((12, 256, 128), BF16),
            pltpu.VMEM((256, D), BF16),
            pltpu.VMEM((4, 96, D + 128), F32),
            pltpu.VMEM((8, ROWS), F32),
        ],
    )
    return pl.pallas_call(
        term_kv_kernel,
        grid_spec=grid_spec,
        out_shape=[
            jax.ShapeDtypeStruct((2, 96, D + 128), F32),
            jax.ShapeDtypeStruct((2, 96, D + 128), BF16),
        ],
        compiler_params=params(11),
        cost_estimate=cost(5),
        name="term_kv",
    )(xs, cs, tokf, merged, *dkvs, w_kv)


def grad_tokens_kernel(x_ref, d0, d1, d2, d3, k0, k1, k2, k3, wq_ref, wkv_ref, wm_ref, out_ref, tiles, dkv, dqs, back):
    x = x_ref[0]
    for e, (q, k) in enumerate(((d0, k0), (d1, k1), (d2, k2), (d3, k3))):
        group = (x + 4 - e) % 4
        dqs[group] = q[0]
        for h in range(3):
            tiles[group * 3 + h] = k[0, h]

    def put(at, value):
        dkv[:, pl.ds(at, 128)] = value

    natural(lambda h: tiles[h], CELLS, put)
    dq = jnp.concatenate([dqs[g].astype(F32).T.astype(BF16) for g in range(4)], axis=1)
    full = mm(dq, wq_ref[...], ((1,), (1,)))
    dmerged = mm(dkv[...], wkv_ref[...], ((1,), (1,)))
    for k in range(12):
        lanes = pl.ds(128 * k, 128)
        back[k] = full[:, 128 * k : 128 * k + 128]
        for t in range(4):
            at = pl.ds(t, CELLS, stride=4)
            back[k, at, :] = back[k, at, :] + wm_ref[t : t + 1, lanes] * dmerged[:, 128 * k : 128 * k + 128]
        out_ref[0, :, lanes] = back[k].astype(BF16)


def grad_of_tokens(xs, dqs, dkvs, w_query, w_kv, w_merge):
    spec = lambda shape: pl.BlockSpec(shape, lambda i, x: (0,) * len(shape))
    grid_spec = pltpu.PrefetchScalarGridSpec(
        num_scalar_prefetch=1,
        grid=(1,),
        in_specs=[pl.BlockSpec((1, GROUP, TOK), lambda i, x: (x[0], 0, 0))] * 4
        + [pl.BlockSpec((1, 3, CELLS, 128), lambda i, x: (x[0], 0, 0, 0))] * 4
        + [spec((D, HD)), spec((D, D)), spec((4, D))],
        out_specs=spec((1, TOK, D)),
        scratch_shapes=[
            pltpu.VMEM((12, CELLS, 128), BF16),
            pltpu.VMEM((CELLS, D), BF16),
            pltpu.VMEM((4, GROUP, TOK), BF16),
            pltpu.VMEM((12, TOK, 128), F32),
        ],
    )
    return pl.pallas_call(
        grad_tokens_kernel,
        grid_spec=grid_spec,
        out_shape=jax.ShapeDtypeStruct((1, TOK, D), BF16),
        compiler_params=params(56),
        cost_estimate=cost(6),
        name="grad_tokens",
    )(xs, *dqs, *dkvs, w_query, w_kv, w_merge)


def spread_x(parts):
    return [parts[0]] + [lax.ppermute(parts[k], "seq", X_SHIFT[k]) for k in range(1, 4)]


def after(value, earlier):
    return lax.optimization_barrier((value, earlier))[0]


def core_sum(keep, send, y):
    got = lax.ppermute(send, "seq", CORE_SWAP)
    summed = keep + got.astype(F32)
    mine = lax.dynamic_index_in_dim(summed, y, 0, False)
    theirs = lax.dynamic_index_in_dim(summed, 1 - y, 0, False).astype(BF16)
    return mine, theirs


def on_device(tokens, keep_index, d_out, w_query, w_kv, w_merge):
    own = tokens[0]
    place = lax.axis_index("seq")
    x = place // 4
    y = (place // 2) % 2
    c = place % 2
    xs = x.reshape(1)
    cs = c.reshape(1)
    parts = keyval(xs, keep_index[0], own, w_merge, w_kv)
    got_kv = spread_x(parts)
    q_parts = queries(xs, keep_index, own, w_query, d_out[0])
    got_kv, q_parts = lax.optimization_barrier((got_kv, q_parts))
    unit = jnp.stack(got_kv)
    qs = spread_x(q_parts)
    unit_c = lax.ppermute(unit, "seq", CORE_SWAP)
    unit_y = lax.ppermute(unit, "seq", Y_SWAP)
    unit_cy = lax.ppermute(unit_y, "seq", CORE_SWAP)

    held = own
    slices = [lax.dynamic_slice(held, (0, ROWS * ((x + k) % 4)), (TOK, ROWS)) for k in range(4)]
    toks = spread_x(after(slices, qs[1]))

    a0, a1, a2, a3, dq, keep, send = attention(xs, qs, [unit, unit_y, unit_c, unit_cy])
    dq, keep, send, toks = lax.optimization_barrier((dq, keep, send, toks))
    dqs = [dq] + [lax.ppermute(dq, "seq", X_SHIFT[k]) for k in range(1, 4)]
    core = lax.ppermute(send, "seq", CORE_SWAP)
    other = (keep[:, 256:] + core[:, 256:].astype(F32)).astype(BF16)
    from_y = lax.ppermute(other, "seq", Y_SWAP)
    taps, weights = after((w_merge, w_kv), other)
    taps = lax.dynamic_slice(taps, (0, ROWS * x), (4, ROWS))
    weights = lax.dynamic_slice(weights, (ROWS * x, 0), (ROWS, D))
    tables = key_tables(after(qs, other))
    dkv = finish_dkv(xs, tables, keep, core, from_y)
    dkvs = [dkv] + [lax.ppermute(dkv, "seq", X_SHIFT[k]) for k in range(1, 4)]

    keep_q, send_q, tokf, unit_merged = term_q(xs, cs, toks, after(dqs, dkv), taps)
    keep_kv, send_kv = term_kv(xs, cs, tokf, unit_merged, dkvs, weights)
    mine_q, theirs_q = core_sum(keep_q, after(send_q, dkv), y)

    mine, theirs = core_sum(keep_kv, send_kv, y)
    theirs_q = after(theirs_q, theirs)
    got_q = lax.ppermute(theirs_q, "seq", Y_SWAP)
    got = lax.ppermute(theirs, "seq", Y_SWAP)
    grads = grad_of_tokens(xs, after(dqs, (theirs, theirs_q)), dkvs, w_query, w_kv, w_merge)
    got, got_q = after((got, got_q), grads)
    total = mine + got.astype(F32)
    total = total.astype(BF16)
    m = jnp.broadcast_to(total[None, :24, D:], (8, 24, 128))
    total = total[:, :D].reshape(4, 24, 2, 768).transpose(0, 2, 1, 3).reshape(8, 24, 768)
    total_q = (mine_q + got_q.astype(F32)).astype(BF16)
    total_q = total_q.reshape(4, 24, 2, 384).transpose(0, 2, 1, 3).reshape(8, 24, 384)
    chunks = jnp.concatenate([total_q, total, m], axis=2)
    shards = lax.all_to_all(chunks, "dp", 0, 0, axis_index_groups=Z_GROUPS)
    a1, a2, a3 = after((a1, a2, a3), chunks)
    back = [a0] + [lax.ppermute(a, "seq", X_SHIFT[4 - k]) for k, a in ((1, a1), (2, a2), (3, a3))]
    order = jnp.stack(back)
    att = jnp.concatenate([lax.dynamic_index_in_dim(order, (g + 4 - x) % 4, 0, False) for g in range(4)], axis=0)
    attended = att.T

    shard = jnp.sum(shards.astype(F32), axis=0).astype(BF16)
    pair = lax.ppermute(shard, "dp", YLO_SWAP)
    shard = shard.astype(F32) + pair.astype(F32)
    grad_m = shard[:4, 1152 : 1152 + 96]
    final = shard[:, :1152].astype(BF16)
    final = lax.all_to_all(jnp.broadcast_to(final[None], (8, 24, 1152)), "dp", 0, 0, axis_index_groups=Z_GROUPS)
    final = final.reshape(4, 2, 24, 1152).transpose(0, 2, 1, 3)
    grad_q = final[..., :384].reshape(96, HD).astype(F32)
    grad_kv = final[..., 384:].reshape(96, D).astype(F32)
    return attended[None], grads, grad_q, grad_kv, grad_m


def solution(mesh):
    placed = (P("dp", "seq", None), P("dp", "seq"), P("dp", "seq", None), P(), P(), P())
    return jax.shard_map(
        on_device,
        mesh=mesh,
        in_specs=placed,
        out_specs=(
            P("dp", "seq", None),
            P("dp", "seq", None),
            P("seq", None),
            P("seq", None),
            P(None, "seq"),
        ),
        check_vma=False,
    )
```
